32 devices in a mesh: sec: 2 (over core), row: 4 (over y, x), col: 4 (over z).
Axes of the slice: x: 2, y: 2, z: 4, core: 2. Of those that a mesh axis runs over, the one named last changes fastest.
Arguments:
- leaf_rhs: bfloat16 [2, 4, 1, 4, 128, 256], P('sec', 'row', None, 'col'), may hold values from -6 to 6
- sep_rhs: bfloat16 [2, 4, 4, 128, 256], P('sec', 'row', 'col'), may hold values from -6 to 6
- top_rhs: bfloat16 [4, 4, 128, 256], P('row', 'col'), may hold values from -6 to 6
- leaf_inv: float32 [2, 4, 1, 4, 128, 128], P('sec', 'row', None, 'col'), may hold values from -1 to 3, as said below
- sep_inv: float32 [2, 4, 4, 128, 128], P('sec', 'row', 'col'), may hold values from -1 to 3, as said below
- top_inv: float32 [4, 4, 128, 128], P('row', 'col'), may hold values from -1 to 3, as said below
- sep_leaf: bfloat16 [2, 4, 4, 128, 4, 1, 4, 128], P('sec', 'row', None, None, None, None, 'col'), may hold values from -0.1875 to 0.1875
- top_leaf: bfloat16 [2, 4, 4, 128, 4, 1, 4, 128], P('sec', 'row', None, None, None, None, 'col'), may hold values from -0.125 to 0.125
- top_sep: bfloat16 [2, 4, 4, 128, 4, 4, 128], P('sec', 'row', None, None, None, 'col'), may hold values from -0.125 to 0.125
- sep_leaf_mask: int32 [2, 4, 4, 4, 1, 4], P('sec', 'row', None, None, None, 'col'), may hold values 0 or 1
- top_leaf_mask: int32 [2, 4, 4, 4, 1, 4], P('sec', 'row', None, None, None, 'col'), may hold values 0 or 1
- top_sep_mask: int32 [2, 4, 4, 4, 4], P('sec', 'row', None, None, 'col'), may hold values 0 or 1
Outputs:
- leaf_x: float32 [2, 4, 1, 4, 128, 256], P('sec', 'row', None, 'col')
- sep_x: float32 [2, 4, 4, 128, 256], P('sec', 'row', 'col')
- top_x: float32 [4, 4, 128, 256], P('row', 'col')
The draws below stay inside these ranges and needn't reach their ends.
Inputs may be any that keep to these rules, and one draw needn't show every extreme that they name: `leaf_inv`: every 128 x 128 block is lower triangular with positive diagonal. `sep_inv`: every 128 x 128 block is lower triangular with positive diagonal. `top_inv`: every 128 x 128 block is lower triangular with positive diagonal.
All inputs are finite; a program needn't handle non-finite values. No bound on the sum of `sep_leaf_mask` or of `top_leaf_mask` or of `top_sep_mask` on one device may be relied on, other than what follows from the above.
Results may differ from the reference program's by a relative error of at most 0.0036.
Values may be sent and summed in bfloat16 or wider, within the bound.
No kernel may reach another device: no remote copies, remote signals or barrier semaphores. Data moves between devices by JAX's collectives and lax.ppermute only.
A program may use at most 128 MiB of HBM per device.

```python
import math
import jax
import jax.numpy as jnp
from jax import lax

W = 128
NRHS = 256
LEAF_DEV = 1
NLEAF = 16
NSEP = 16
N_SEC = 2
N_ROW = 4
N_COL = 4


def triangle_blocks(key, leading):
    key_diag, key_below = jax.random.split(key)
    full_shape = leading + (W, W)
    lower_part = (lax.broadcasted_iota(jnp.int32, (W, W), 0) > lax.broadcasted_iota(jnp.int32, (W, W), 1)).astype(jnp.float32)
    on_diag = (lax.broadcasted_iota(jnp.int32, (W, W), 0) == lax.broadcasted_iota(jnp.int32, (W, W), 1)).astype(jnp.float32)
    diagonal = jax.random.uniform(key_diag, leading + (W, 1), jnp.float32, 0.6, 1.5)
    spread = jnp.clip(jax.random.normal(key_below, full_shape, jnp.float32), -4.0, 4.0) * (0.6 / math.sqrt(W))
    return spread * lower_part + diagonal * on_diag


def draw_leaf_inv(key, part):
    return triangle_blocks(key, (N_SEC, N_ROW, LEAF_DEV, N_COL))


def draw_sep_inv(key, part):
    return triangle_blocks(key, (N_SEC, N_ROW, N_COL))


def draw_top_inv(key, part):
    return triangle_blocks(key, (N_ROW, N_COL))


def place_ends(drawn, stream_key, smallest, high):
    spot = [jax.random.randint(jax.random.fold_in(stream_key, axis), (), 0, length) for axis, length in enumerate(drawn.shape)]
    main_axis = drawn.shape.index(max(drawn.shape))
    beside = spot[:main_axis] + [(spot[main_axis] + 1) % drawn.shape[main_axis]] + spot[main_axis + 1:]
    return drawn.at[tuple(spot)].set(smallest).at[tuple(beside)].set(high)


def block_scale(rng, extent, cuts, least, top_value):
    factor_of = 1.0
    for position, parts in cuts:
        draws = jax.random.uniform(jax.random.fold_in(jax.random.fold_in(rng, 6), position), (parts,), jnp.float32, least / len(cuts), top_value / len(cuts))
        factor_of = factor_of * jnp.repeat(jnp.exp(draws), extent[position] // parts).reshape((-1,) + (1,) * (len(extent) - 1 - position))
    return factor_of


def scatter_about(rng, shape, width, limit, cuts=(), dtype=jnp.bfloat16):
    result = jax.random.normal(rng, shape, jnp.float32) * width
    if len(cuts) > 0:
        result = block_scale(rng, shape, cuts, -0.22, 0.18) * result
    return jnp.clip(result, min=-limit, max=limit).astype(dtype)


def setup_inputs(seed: int = 0) -> dict:
    streams_of = jax.random.split(jax.random.key(seed), 13)
    leaf_rhs = scatter_about(streams_of[0], (N_SEC, N_ROW, LEAF_DEV, N_COL, W, NRHS), 1.0, 6.0, ((0, 2), (1, 4), (3, 4)))
    sep_rhs = scatter_about(streams_of[1], (N_SEC, N_ROW, N_COL, W, NRHS), 1.0, 6.0, ((0, 2), (1, 4), (2, 4)))
    top_rhs = scatter_about(streams_of[2], (N_ROW, N_COL, W, NRHS), 1.0, 6.0, ((0, 4), (1, 4)))
    leaf_inv = draw_leaf_inv(jax.random.fold_in(streams_of[12], 71), 0)
    sep_inv = draw_sep_inv(jax.random.fold_in(streams_of[12], 71), 0)
    top_inv = draw_top_inv(jax.random.fold_in(streams_of[12], 71), 0)
    sep_leaf = scatter_about(streams_of[6], (N_SEC, N_ROW, N_COL, W, N_ROW, LEAF_DEV, N_COL, W), (W * NLEAF // 2) ** -0.5, 0.1875, ((0, 2), (1, 4), (6, 4)))
    top_leaf = scatter_about(streams_of[7], (N_SEC, N_ROW, N_COL, W, N_ROW, LEAF_DEV, N_COL, W), (W * NLEAF) ** -0.5, 0.125, ((0, 2), (1, 4), (6, 4)))
    top_sep = scatter_about(streams_of[8], (N_SEC, N_ROW, N_COL, W, N_ROW, N_COL, W), (W * NSEP) ** -0.5, 0.125, ((0, 2), (1, 4), (5, 4)))
    sep_leaf_mask = place_ends((jax.random.randint(streams_of[9], (N_SEC, N_ROW, N_COL, N_ROW, LEAF_DEV, N_COL), 0, 2) < 1).astype(jnp.int32), jax.random.fold_in(streams_of[9], 1), 0, 1)
    top_leaf_mask = place_ends((jax.random.randint(streams_of[10], (N_SEC, N_ROW, N_COL, N_ROW, LEAF_DEV, N_COL), 0, 2) < 1).astype(jnp.int32), jax.random.fold_in(streams_of[10], 1), 0, 1)
    top_sep_mask = place_ends((jax.random.randint(streams_of[11], (N_SEC, N_ROW, N_COL, N_ROW, N_COL), 0, 2) < 1).astype(jnp.int32), jax.random.fold_in(streams_of[11], 1), 0, 1)
    return {"leaf_rhs": leaf_rhs, "sep_rhs": sep_rhs, "top_rhs": top_rhs, "leaf_inv": leaf_inv, "sep_inv": sep_inv, "top_inv": top_inv, "sep_leaf": sep_leaf, "top_leaf": top_leaf, "top_sep": top_sep, "sep_leaf_mask": sep_leaf_mask, "top_leaf_mask": top_leaf_mask, "top_sep_mask": top_sep_mask}


def lower_apply(inverse, right_side):
    return jnp.einsum("...ab,...bn->...an", inverse, right_side, precision=lax.Precision.HIGHEST)


def upper_apply(inverse, right_side):
    return jnp.einsum("...ba,...bn->...an", inverse, right_side, precision=lax.Precision.HIGHEST)


def reference(leaf_rhs, sep_rhs, top_rhs, leaf_inv, sep_inv, top_inv, sep_leaf, top_leaf, top_sep, sep_leaf_mask, top_leaf_mask, top_sep_mask):
    node_rows = N_ROW * N_COL * W
    leaf_rows = N_ROW * LEAF_DEV * N_COL * W
    contract = (((0,), (0,)), ((), ()))

    def masked_leaf(tile_set, pattern):
        weights = pattern.astype(jnp.bfloat16)[:, :, None, :, :, :, None]
        return (tile_set * weights).reshape(node_rows, leaf_rows)

    def masked_cross(tile_set, pattern):
        weights = pattern.astype(jnp.bfloat16)[:, :, None, :, :, None]
        return (tile_set * weights).reshape(node_rows, node_rows)

    def forward(section):
        rhs_leaf, inv_leaf, rhs_sep, inv_sep, tiles_sl, tiles_tl, tiles_ts, mask_sl, mask_tl, mask_ts = section
        leaf_y = lower_apply(inv_leaf, rhs_leaf.astype(jnp.float32))
        leaf_flat = leaf_y.astype(jnp.bfloat16).reshape(leaf_rows, NRHS)
        sep_sum = jnp.dot(masked_leaf(tiles_sl, mask_sl), leaf_flat, preferred_element_type=jnp.float32)
        sep_y = lower_apply(inv_sep, rhs_sep.astype(jnp.float32) - sep_sum.reshape(N_ROW, N_COL, W, NRHS))
        sep_flat = sep_y.astype(jnp.bfloat16).reshape(node_rows, NRHS)
        top_part = jnp.dot(masked_leaf(tiles_tl, mask_tl), leaf_flat, preferred_element_type=jnp.float32)
        top_part = top_part + jnp.dot(masked_cross(tiles_ts, mask_ts), sep_flat, preferred_element_type=jnp.float32)
        return leaf_y, sep_y, top_part

    leaf_y, sep_y, top_parts = lax.map(forward, (leaf_rhs, leaf_inv, sep_rhs, sep_inv, sep_leaf, top_leaf, top_sep, sep_leaf_mask, top_leaf_mask, top_sep_mask))
    top_sum = jnp.sum(top_parts, axis=0).reshape(N_ROW, N_COL, W, NRHS)
    top_y = lower_apply(top_inv, top_rhs.astype(jnp.float32) - top_sum)
    top_x = upper_apply(top_inv, top_y)
    top_flat = top_x.astype(jnp.bfloat16).reshape(node_rows, NRHS)

    def backward(section):
        sep_y_s, leaf_y_s, inv_sep, inv_leaf, tiles_sl, tiles_tl, tiles_ts, mask_sl, mask_tl, mask_ts = section
        sep_t = lax.dot_general(masked_cross(tiles_ts, mask_ts), top_flat, contract, preferred_element_type=jnp.float32)
        sep_x = upper_apply(inv_sep, sep_y_s - sep_t.reshape(N_ROW, N_COL, W, NRHS))
        sep_flat = sep_x.astype(jnp.bfloat16).reshape(node_rows, NRHS)
        leaf_t = lax.dot_general(masked_leaf(tiles_sl, mask_sl), sep_flat, contract, preferred_element_type=jnp.float32)
        leaf_t = leaf_t + lax.dot_general(masked_leaf(tiles_tl, mask_tl), top_flat, contract, preferred_element_type=jnp.float32)
        leaf_x = upper_apply(inv_leaf, leaf_y_s - leaf_t.reshape(N_ROW, LEAF_DEV, N_COL, W, NRHS))
        return leaf_x, sep_x

    leaf_x, sep_x = lax.map(backward, (sep_y, leaf_y, sep_inv, leaf_inv, sep_leaf, top_leaf, top_sep, sep_leaf_mask, top_leaf_mask, top_sep_mask))
    return leaf_x, sep_x, top_x
```

```python
import jax
import jax.numpy as jnp
from jax import lax
from jax.sharding import PartitionSpec as P

BF = jnp.bfloat16
F32 = jnp.float32
HI = lax.Precision.HIGHEST


def is_direct(n):
    return n in (1, 2, 4)


def swap(values, axis, n, step):
    return lax.ppermute(values, axis, [(i, i ^ step) for i in range(n)])


def partner_order(values, axis_name, n, dim):
    if not is_direct(n):
        return values
    me = lax.axis_index(axis_name)
    return jnp.concatenate(
        [lax.dynamic_slice_in_dim(values, me ^ d, 1, dim) for d in range(n)], axis=dim
    )


def gather(values, axis, n):
    if not is_direct(n):
        return lax.all_gather(values, axis, axis=0, tiled=True)
    return jnp.concatenate([values] + [swap(values, axis, n, d) for d in range(1, n)], axis=0)


def scatter_sum(block_fn, axis, n):
    if not is_direct(n):
        stacked = jnp.stack([block_fn(d) for d in range(n)])
        return lax.psum_scatter(stacked, axis, scatter_dimension=0, tiled=True)[0]
    got = [swap(block_fn(d).astype(BF), axis, n, d) for d in range(1, n)]
    total = block_fn(0)
    for piece in got:
        total = total + piece.astype(F32)
    return total


def dot(a, b):
    return jnp.dot(a, b, preferred_element_type=F32)


def dot_t(a, b):
    return lax.dot_general(a, b, (((0,), (0,)), ((), ())), preferred_element_type=F32)


def lower_apply(inverse, right_side):
    return jnp.einsum("...ab,...bn->...an", inverse, right_side, precision=HI)


def upper_apply(inverse, right_side):
    return jnp.einsum("...ba,...bn->...an", inverse, right_side, precision=HI)


def make_body(n_sec, n_row, n_col):
    def body(leaf_rhs, sep_rhs, top_rhs, leaf_inv, sep_inv, top_inv,
             sep_leaf, top_leaf, top_sep, sep_leaf_mask, top_leaf_mask, top_sep_mask):
        leaf_count, width, cols = leaf_rhs.shape[2], leaf_rhs.shape[4], leaf_rhs.shape[5]
        span = leaf_count * width
        half = cols // n_sec
        sec = lax.axis_index("sec")

        def tiles(values, mask):
            masked = values * mask.astype(BF)[:, None, :, :, None]
            masked = masked.reshape(n_col, width, n_row, -1)
            masked = partner_order(partner_order(masked, "col", n_col, 0), "row", n_row, 2)
            return masked.reshape(n_col, width, -1)

        sl = tiles(sep_leaf[0, 0, :, :, :, :, 0], sep_leaf_mask[0, 0, :, :, :, 0])
        tl = tiles(top_leaf[0, 0, :, :, :, :, 0], top_leaf_mask[0, 0, :, :, :, 0])
        ts = tiles(top_sep[0, 0, :, :, :, None, 0], top_sep_mask[0, 0, :, :, None, 0])

        leaf_y = lower_apply(leaf_inv[0, 0, :, 0], leaf_rhs[0, 0, :, 0].astype(F32))
        leaf_col = gather(leaf_y.astype(BF).reshape(span, cols), "row", n_row)
        sep_sum = scatter_sum(lambda d: dot(sl[d], leaf_col), "col", n_col)
        sep_y = lower_apply(sep_inv[0, 0, 0], sep_rhs[0, 0, 0].astype(F32) - sep_sum)
        sep_col = gather(sep_y.astype(BF), "row", n_row)

        top_part = dot(ts.reshape(n_col * width, -1), sep_col) + dot(tl.reshape(n_col * width, -1), leaf_col)
        if n_sec == 2:
            mine = lax.dynamic_slice_in_dim(top_part, sec * half, half, 1)
            other = lax.dynamic_slice_in_dim(top_part, (1 - sec) * half, half, 1).astype(BF)
            top_half = mine + swap(other, "sec", 2, 1).astype(F32)
        else:
            top_half = lax.psum_scatter(top_part, "sec", scatter_dimension=1, tiled=True)
        top_half = top_half.reshape(n_col, width, half)
        top_sum = scatter_sum(lambda d: top_half[d], "col", n_col)
        rhs_half = lax.dynamic_slice_in_dim(top_rhs[0, 0], sec * half, half, 1).astype(F32)
        top_y = lower_apply(top_inv[0, 0], rhs_half - top_sum)
        top_xh = upper_apply(top_inv[0, 0], top_y)
        top_xb = gather(top_xh.astype(BF), "col", n_col)
        if n_sec == 2:
            other = swap(top_xb, "sec", 2, 1)
            low = jnp.where(sec == 0, top_xb, other)
            high = jnp.where(sec == 0, other, top_xb)
            top_row = jnp.concatenate([low, high], axis=1)
            other = swap(top_xh, "sec", 2, 1)
            top_x = jnp.concatenate([jnp.where(sec == 0, top_xh, other), jnp.where(sec == 0, other, top_xh)], axis=1)
        else:
            top_row = lax.all_gather(top_xb, "sec", axis=1, tiled=True)
            top_x = lax.all_gather(top_xh, "sec", axis=1, tiled=True)

        ts_flat = ts.reshape(n_col * width, n_row, width)
        sl_flat = sl.reshape(n_col * width, n_row, span)
        tl_flat = tl.reshape(n_col * width, n_row, span)
        sep_t = scatter_sum(lambda d: dot_t(ts_flat[:, d], top_row), "row", n_row)
        sep_x = upper_apply(sep_inv[0, 0, 0], sep_y - sep_t)
        sep_row = gather(sep_x.astype(BF), "col", n_col)
        leaf_t = scatter_sum(
            lambda d: dot_t(sl_flat[:, d], sep_row) + dot_t(tl_flat[:, d], top_row), "row", n_row
        )
        leaf_x = upper_apply(leaf_inv[0, 0, :, 0], leaf_y - leaf_t.reshape(leaf_count, width, cols))
        return leaf_x[None, None, :, None], sep_x[None, None, None], top_x[None, None]

    return body


def solution(mesh):
    in_specs = (
        P("sec", "row", None, "col", None, None),
        P("sec", "row", "col", None, None),
        P("row", "col", None, None),
        P("sec", "row", None, "col", None, None),
        P("sec", "row", "col", None, None),
        P("row", "col", None, None),
        P("sec", "row", None, None, None, None, "col", None),
        P("sec", "row", None, None, None, None, "col", None),
        P("sec", "row", None, None, None, "col", None),
        P("sec", "row", None, None, None, "col"),
        P("sec", "row", None, None, None, "col"),
        P("sec", "row", None, None, "col"),
    )
    out_specs = (
        P("sec", "row", None, "col", None, None),
        P("sec", "row", "col", None, None),
        P("row", "col", None, None),
    )
    body = make_body(mesh.shape["sec"], mesh.shape["row"], mesh.shape["col"])
    return jax.shard_map(body, mesh=mesh, in_specs=in_specs, out_specs=out_specs, check_vma=False)
```

```python
import jax
import jax.numpy as jnp
from jax import lax
from jax.experimental import pallas as pl
from jax.experimental.pallas import tpu as pltpu
from jax.sharding import PartitionSpec as P

BF = jnp.bfloat16
F32 = jnp.float32
HI = lax.Precision.HIGHEST
VMEM = pl.BlockSpec(memory_space=pltpu.VMEM)


def is_direct(n):
    return n in (1, 2, 4)


def swap(values, axis, n, step):
    return lax.ppermute(values, axis, [(i, i ^ step) for i in range(n)])


def gather(values, axis, n):
    if is_direct(n):
        return [values] + [swap(values, axis, n, d) for d in range(1, n)]
    return [lax.all_gather(values, axis, axis=0, tiled=True)]


def scatter_sum(blocks, axis, n):
    if is_direct(n):
        return [blocks[0]] + [swap(blocks[d], axis, n, d) for d in range(1, n)]
    return [lax.psum_scatter(blocks[0], axis, scatter_dimension=0, tiled=True)]


def nbytes(shape, dtype):
    size = jnp.dtype(dtype).itemsize
    for extent in shape:
        size *= extent
    return size


def call(kernel, outs, args, scratch=(), flops=0):
    total = sum(nbytes(s, t) for s, t in list(outs) + list(scratch)) + sum(nbytes(a.shape, a.dtype) for a in args)
    return pl.pallas_call(
        kernel,
        out_shape=tuple(jax.ShapeDtypeStruct(s, t) for s, t in outs),
        in_specs=[VMEM] * len(args),
        out_specs=(VMEM,) * len(outs),
        scratch_shapes=[pltpu.VMEM(s, t) for s, t in scratch],
        compiler_params=pltpu.CompilerParams(vmem_limit_bytes=total + (6 << 20)),
        cost_estimate=pl.CostEstimate(flops=flops, bytes_accessed=total, transcendentals=0),
    )(*args)


def place(n, axis):
    if not is_direct(n):
        return lambda d: d
    me = lax.axis_index(axis)
    return lambda d: me ^ d


def rows(index, size):
    return pl.ds(pl.multiple_of(index * size, size), size)


def dot(a, b):
    return jnp.dot(a, b, preferred_element_type=F32)


def dot_t(a, b):
    return lax.dot_general(a, b, (((0,), (0,)), ((), ())), preferred_element_type=F32)


def apply_lower(inverse, right_side):
    return jnp.dot(inverse, right_side, precision=HI, preferred_element_type=F32)


def apply_upper(inverse, right_side):
    return lax.dot_general(
        inverse, right_side, (((0,), (0,)), ((), ())), precision=HI, preferred_element_type=F32
    )


def total_of(refs):
    total = refs[0][...].astype(F32)
    for ref in refs[1:]:
        total = total + ref[...].astype(F32)
    return total


def lay_out(pieces, buf, n, axis):
    if not is_direct(n):
        buf[...] = pieces[0][...]
        return
    at = place(n, axis)
    size = pieces[0].shape[0]
    for d, piece in enumerate(pieces):
        buf[rows(at(d), size), :] = piece[...]


def block_outs(n, size, cols):
    if is_direct(n):
        return [((size, cols), F32)] + [((size, cols), BF)] * (n - 1)
    return [((n * size, cols), F32)]


def emit_blocks(term, outs, n, axis):
    at = place(n, axis)
    if is_direct(n):
        for d in list(range(1, n)) + [0]:
            outs[d][...] = term(at(d)).astype(outs[d].dtype)
    else:
        size = outs[0].shape[0] // n
        for d in range(n):
            outs[0][pl.ds(d * size, size), :] = term(d)


def leaf_first(leaf_inv, leaf_rhs):
    count, width, cols = leaf_rhs.shape

    def kernel(inv_ref, rhs_ref, y_ref, yb_ref):
        for m in range(count):
            y = apply_lower(inv_ref[m], rhs_ref[m].astype(F32))
            y_ref[pl.ds(m * width, width), :] = y
            yb_ref[pl.ds(m * width, width), :] = y.astype(BF)

    shape = (count * width, cols)
    return call(kernel, [(shape, F32), (shape, BF)], [leaf_inv, leaf_rhs])


def forward_blocks(tiles, pieces, n_row, n_col, width):
    cols = pieces[0].shape[1]
    depth = tiles.shape[1]
    count = len(pieces)

    def kernel(*refs):
        tile_ref, piece_refs, outs = refs[0], refs[1 : 1 + count], refs[1 + count : -1]
        buf = refs[-1]
        lay_out(piece_refs, buf, n_row, "row")
        emit_blocks(lambda i: dot(tile_ref[rows(i, width), :], buf[...]), outs, n_col, "col")

    outs = block_outs(n_col, width, cols) + [((depth, cols), BF)]
    got = call(kernel, outs, [tiles, *pieces], flops=2 * tiles.shape[0] * depth * cols)
    return got[:-1], got[-1]


def plain_product(tiles, values, transposed):
    cols = values.shape[1]
    product = dot_t if transposed else dot

    def kernel(tile_ref, value_ref, out_ref):
        out_ref[...] = product(tile_ref[...], value_ref[...])

    shape = (tiles.shape[1] if transposed else tiles.shape[0], cols)
    return call(kernel, [(shape, F32)], [tiles, values], flops=2 * tiles.shape[0] * tiles.shape[1] * cols)[0]


def solve_forward(sums, right_side, inverse):
    count = len(sums)

    def kernel(*refs):
        rhs_ref, inv_ref, y_ref, yb_ref = refs[count:]
        y = apply_lower(inv_ref[...], rhs_ref[...].astype(F32) - total_of(refs[:count]))
        y_ref[...] = y
        yb_ref[...] = y.astype(BF)

    shape = right_side.shape
    return call(kernel, [(shape, F32), (shape, BF)], [*sums, right_side, inverse])


def top_halves(tiles, pieces, leaf_part, n_row):
    cols = pieces[0].shape[1]
    half = cols // 2
    count = len(pieces)

    def kernel(*refs):
        tile_ref, piece_refs = refs[0], refs[1 : 1 + count]
        part_ref, mine_ref, other_ref, buf = refs[1 + count :]
        lay_out(piece_refs, buf, n_row, "row")
        sec = lax.axis_index("sec")
        for out_ref, which in ((other_ref, 1 - sec), (mine_ref, sec)):
            columns = rows(which, half)
            out = part_ref[:, columns] + dot(tile_ref[...], buf[:, columns])
            out_ref[...] = out.astype(out_ref.dtype)

    shape = (tiles.shape[0], half)
    return call(
        kernel,
        [(shape, F32), (shape, F32)],
        [tiles, *pieces, leaf_part],
        scratch=[((tiles.shape[1], cols), BF)],
        flops=2 * tiles.shape[0] * tiles.shape[1] * cols,
    )


def add_sections(mine, other, n_col, width):
    half = mine.shape[1]

    def kernel(mine_ref, other_ref, *outs):
        emit_blocks(lambda i: mine_ref[rows(i, width), :] + other_ref[rows(i, width), :], outs, n_col, "col")

    return call(kernel, block_outs(n_col, width, half), [mine, other])


def solve_top(sums, right_side, inverse):
    count = len(sums)
    half = right_side.shape[1] // 2

    def kernel(*refs):
        rhs_ref, inv_ref, x_ref, xb_ref = refs[count:]
        mine = rhs_ref[:, rows(lax.axis_index("sec"), half)].astype(F32)
        y = apply_lower(inv_ref[...], mine - total_of(refs[:count]))
        x = apply_upper(inv_ref[...], y)
        x_ref[...] = x
        xb_ref[...] = x.astype(BF)

    shape = (right_side.shape[0], half)
    return call(kernel, [(shape, F32), (shape, BF)], [*sums, right_side, inverse])


def stack_pieces(pieces, n, axis):
    if not is_direct(n):
        return pieces[0]

    def kernel(*refs):
        lay_out(refs[:-1], refs[-1], n, axis)

    shape = (n * pieces[0].shape[0], pieces[0].shape[1])
    return call(kernel, [(shape, BF)], list(pieces))[0]


def join_halves(mine, other):
    half = mine.shape[1]

    def kernel(mine_ref, other_ref, out_ref):
        sec = lax.axis_index("sec")
        out_ref[:, rows(sec, half)] = mine_ref[...]
        out_ref[:, rows(1 - sec, half)] = other_ref[...]

    return call(kernel, [((mine.shape[0], 2 * half), mine.dtype)], [mine, other])[0]


def top_back_blocks(tiles, mine, other, n_row, width):
    half = mine.shape[1]

    def kernel(tile_ref, mine_ref, other_ref, *outs):
        buf = outs[-1]
        sec = lax.axis_index("sec")
        buf[:, rows(sec, half)] = mine_ref[...]
        buf[:, rows(1 - sec, half)] = other_ref[...]
        emit_blocks(lambda i: dot_t(tile_ref[:, rows(i, width)], buf[...]), outs[:-1], n_row, "row")

    outs = block_outs(n_row, width, 2 * half) + [((mine.shape[0], 2 * half), BF)]
    got = call(kernel, outs, [tiles, mine, other], flops=4 * tiles.shape[0] * tiles.shape[1] * half)
    return got[:-1], got[-1]


def back_blocks(tiles, pieces, top_part, n_row, n_col, span):
    cols = pieces[0].shape[1]
    count = len(pieces)

    def kernel(*refs):
        tile_ref, piece_refs, part_ref = refs[0], refs[1 : 1 + count], refs[1 + count]
        outs, buf = refs[2 + count : -1], refs[-1]
        lay_out(piece_refs, buf, n_col, "col")
        emit_blocks(
            lambda i: part_ref[rows(i, span), :] + dot_t(tile_ref[:, rows(i, span)], buf[...]),
            outs, n_row, "row",
        )

    return call(
        kernel,
        block_outs(n_row, span, cols),
        [tiles, *pieces, top_part],
        scratch=[((tiles.shape[0], cols), BF)],
        flops=2 * tiles.shape[0] * tiles.shape[1] * cols,
    )


def solve_back(sums, right_side, inverse):
    count = len(sums)
    blocks, width = inverse.shape[:2]
    shape = right_side.shape

    def kernel(*refs):
        y_ref, inv_ref, x_ref, xb_ref = refs[count:]
        rest = y_ref[...] - total_of(refs[:count])
        for m in range(blocks):
            x = apply_upper(inv_ref[m], rest[m * width : (m + 1) * width])
            x_ref[pl.ds(m * width, width), :] = x
            xb_ref[pl.ds(m * width, width), :] = x.astype(BF)

    return call(kernel, [(shape, F32), (shape, BF)], [*sums, right_side, inverse])


def solve_last(sums, right_side, inverse):
    count = len(sums)
    blocks, width = inverse.shape[:2]

    def kernel(*refs):
        y_ref, inv_ref, x_ref = refs[count:]
        rest = y_ref[...] - total_of(refs[:count])
        for m in range(blocks):
            x_ref[pl.ds(m * width, width), :] = apply_upper(inv_ref[m], rest[m * width : (m + 1) * width])

    return call(kernel, [(right_side.shape, F32)], [*sums, right_side, inverse])[0]


def make_body(n_row, n_col):
    def body(leaf_rhs, sep_rhs, top_rhs, leaf_inv, sep_inv, top_inv,
             sep_leaf, top_leaf, top_sep, sep_leaf_mask, top_leaf_mask, top_sep_mask):
        leaf_count, width, cols = leaf_rhs.shape[2], leaf_rhs.shape[4], leaf_rhs.shape[5]
        span = leaf_count * width

        def tiles(values, mask):
            masked = values * mask.astype(BF)[:, None, :, :, None]
            return masked.reshape(n_col * width, -1)

        leaf_y, leaf_yb = leaf_first(leaf_inv[0, 0, :, 0], leaf_rhs[0, 0, :, 0])
        sl = tiles(sep_leaf[0, 0, :, :, :, :, 0], sep_leaf_mask[0, 0, :, :, :, 0])
        blocks, leaf_col = forward_blocks(sl, gather(leaf_yb, "row", n_row), n_row, n_col, width)
        sums = scatter_sum(blocks, "col", n_col)
        top_leaf, top_sep, top_leaf_mask, top_sep_mask, leaf_col = lax.optimization_barrier(
            (top_leaf, top_sep, top_leaf_mask, top_sep_mask, leaf_col)
        )
        tl = tiles(top_leaf[0, 0, :, :, :, :, 0], top_leaf_mask[0, 0, :, :, :, 0])
        ts = tiles(top_sep[0, 0, :, :, :, None, 0], top_sep_mask[0, 0, :, :, None, 0])
        leaf_part = plain_product(tl, leaf_col, False)
        sep_y, sep_yb = solve_forward(sums, sep_rhs[0, 0, 0], sep_inv[0, 0, 0])
        mine, other = top_halves(ts, gather(sep_yb, "row", n_row), leaf_part, n_row)
        blocks = add_sections(mine, swap(other, "sec", 2, 1), n_col, width)
        sums = scatter_sum(blocks, "col", n_col)
        top_xh, top_xhb = solve_top(sums, top_rhs[0, 0], top_inv[0, 0])
        top_stack = stack_pieces(gather(top_xhb, "col", n_col), n_col, "col")
        blocks, top_row = top_back_blocks(ts, top_stack, swap(top_stack, "sec", 2, 1), n_row, width)
        sums = scatter_sum(blocks, "row", n_row)
        top_part = plain_product(tl, top_row, True)
        top_x = join_halves(top_xh, swap(top_xh, "sec", 2, 1))
        sep_x, sep_xb = solve_back(sums, sep_y, sep_inv[0, 0])
        pieces = gather(sep_xb, "col", n_col)
        sums = scatter_sum(back_blocks(sl, pieces, top_part, n_row, n_col, span), "row", n_row)
        leaf_x = solve_last(sums, leaf_y, leaf_inv[0, 0, :, 0])
        return (
            leaf_x.reshape(1, 1, leaf_count, 1, width, cols),
            sep_x[None, None, None],
            top_x[None, None],
        )

    return body


def solution(mesh):
    in_specs = (
        P("sec", "row", None, "col", None, None),
        P("sec", "row", "col", None, None),
        P("row", "col", None, None),
        P("sec", "row", None, "col", None, None),
        P("sec", "row", "col", None, None),
        P("row", "col", None, None),
        P("sec", "row", None, None, None, None, "col", None),
        P("sec", "row", None, None, None, None, "col", None),
        P("sec", "row", None, None, None, "col", None),
        P("sec", "row", None, None, None, "col"),
        P("sec", "row", None, None, None, "col"),
        P("sec", "row", None, None, "col"),
    )
    out_specs = (
        P("sec", "row", None, "col", None, None),
        P("sec", "row", "col", None, None),
        P("row", "col", None, None),
    )
    body = make_body(mesh.shape["row"], mesh.shape["col"])
    return jax.shard_map(body, mesh=mesh, in_specs=in_specs, out_specs=out_specs, check_vma=False)
```

```python
import jax
import jax.numpy as jnp
from jax import lax
from jax.experimental import pallas as pl
from jax.experimental.pallas import tpu as pltpu
from jax.sharding import PartitionSpec as P

BF = jnp.bfloat16
F32 = jnp.float32
VMEM = pl.BlockSpec(memory_space=pltpu.VMEM)
HBM = pl.BlockSpec(memory_space=pltpu.HBM)


def is_direct(n):
    return n in (1, 2, 4)


def swap_all(blocks, axis, n):
    steps = (2, 1, 3) if axis == "col" and n == 4 else range(1, n)
    got = {d: swap(blocks[d], axis, n, d) for d in steps}
    return [got[d] for d in range(1, n)]


def swap(values, axis, n, step):
    return lax.ppermute(values, axis, [(i, i ^ step) for i in range(n)])


def gather(values, axis, n):
    if is_direct(n):
        return [values] + swap_all([values] * n, axis, n)
    return [lax.all_gather(values, axis, axis=0, tiled=True)]


def scatter_sum(blocks, axis, n):
    if is_direct(n):
        return [blocks[0]] + swap_all(blocks, axis, n)
    return [lax.psum_scatter(blocks[0], axis, scatter_dimension=0, tiled=True)]


def nbytes(shape, dtype):
    size = jnp.dtype(dtype).itemsize
    for extent in shape:
        size *= extent
    return size


def call(kernel, outs, args, scratch=(), flops=0, in_specs=None, sems=0):
    total = sum(nbytes(s, t) for s, t in list(outs) + list(scratch)) + sum(nbytes(a.shape, a.dtype) for a in args)
    return pl.pallas_call(
        kernel,
        out_shape=tuple(jax.ShapeDtypeStruct(s, t) for s, t in outs),
        in_specs=in_specs or [VMEM] * len(args),
        out_specs=(VMEM,) * len(outs),
        scratch_shapes=[pltpu.VMEM(s, t) for s, t in scratch] + ([pltpu.SemaphoreType.DMA((sems,))] if sems else []),
        compiler_params=pltpu.CompilerParams(vmem_limit_bytes=total + (6 << 20)),
        cost_estimate=pl.CostEstimate(flops=flops, bytes_accessed=total, transcendentals=0),
    )(*args)


def place(n, axis):
    if not is_direct(n):
        return lambda d: d
    me = lax.axis_index(axis)
    return lambda d: me ^ d


def rows(index, size):
    return pl.ds(pl.multiple_of(index * size, size), size)


def dot(a, b):
    return jnp.dot(a, b, preferred_element_type=F32)


def dot_t(a, b):
    return lax.dot_general(a, b, (((0,), (0,)), ((), ())), preferred_element_type=F32)


def split(values):
    high = values.astype(BF)
    return high, (values - high.astype(F32)).astype(BF)


def apply_split(parts, right_side):
    high, low = split(right_side)
    return dot(parts, jnp.concatenate([high, high, low], axis=0))


def total_of(refs):
    total = refs[0][...].astype(F32)
    for ref in refs[1:]:
        total = total + ref[...].astype(F32)
    return total


def lay_out(pieces, buf, n, axis):
    if not is_direct(n):
        buf[...] = pieces[0][...]
        return
    at = place(n, axis)
    size = pieces[0].shape[0]
    for d, piece in enumerate(pieces):
        buf[rows(at(d), size), :] = piece[...]


def block_outs(n, size, cols):
    if is_direct(n):
        return [((size, cols), F32)] + [((size, cols), BF)] * (n - 1)
    return [((n * size, cols), F32)]


def emit_blocks(term, outs, n, axis):
    at = place(n, axis)
    if is_direct(n):
        for d in list(range(1, n)) + [0]:
            outs[d][...] = term(at(d)).astype(outs[d].dtype)
    else:
        size = outs[0].shape[0] // n
        for d in range(n):
            outs[0][pl.ds(d * size, size), :] = term(d)


def leaf_first(leaf_inv, leaf_rhs):
    count, width, cols = leaf_rhs.shape

    def kernel(inv_hbm, rhs_hbm, y_ref, yb_ref, inv_ref, rhs_ref, sems):
        copies = [
            pltpu.make_async_copy(inv_hbm, inv_ref, sems.at[0]),
            pltpu.make_async_copy(rhs_hbm, rhs_ref, sems.at[1]),
        ]
        for copy in copies:
            copy.start()
        for copy in copies:
            copy.wait()
        for m in range(count):
            high, low = split(inv_ref[m])
            rhs = rhs_ref[m]
            y = dot(jnp.concatenate([high, low], axis=1), jnp.concatenate([rhs, rhs], axis=0))
            y_ref[pl.ds(m * width, width), :] = y
            yb_ref[pl.ds(m * width, width), :] = y.astype(BF)

    shape = (count * width, cols)
    return call(
        kernel,
        [(shape, F32), (shape, BF)],
        [leaf_inv, leaf_rhs],
        scratch=[(leaf_inv.shape, F32), (leaf_rhs.shape, BF)],
        in_specs=[HBM] * 2,
        sems=2,
    )


def mask_tiles(tile_sets, masks, width):
    count = len(masks)
    n_col = masks[0].shape[0]

    def kernel(*refs):
        masks_hbm, tile_refs, outs = refs[:count], refs[count : 2 * count], refs[2 * count : 3 * count]
        mask_refs, sems = refs[3 * count : 4 * count], refs[4 * count]
        copies = [pltpu.make_async_copy(masks_hbm[i], mask_refs[i], sems.at[i]) for i in range(count)]
        for copy in copies:
            copy.start()
        for copy in copies:
            copy.wait()
        for i in range(count):
            for k in range(masks[i].shape[2]):
                weight = jnp.broadcast_to(mask_refs[i][:, :, k : k + 1].astype(F32), (n_col, 1, width)).astype(BF)
                lanes = pl.ds(k * width, width)
                outs[i][:, :, lanes] = tile_refs[i][:, :, lanes] * weight

    return call(
        kernel,
        [(t.shape, BF) for t in tile_sets],
        [*masks, *tile_sets],
        scratch=[(m.shape, m.dtype) for m in masks],
        in_specs=[HBM] * count + [VMEM] * count,
        sems=count,
    )


def split_inverse(inverse):
    blocks, width = inverse.shape[:2]

    def kernel(inv_ref, low_ref, up_ref):
        for m in range(blocks):
            value = inv_ref[m]
            for out_ref, part in ((low_ref, value), (up_ref, value.T)):
                high, low = split(part)
                out_ref[m, :, pl.ds(0, width)] = high
                out_ref[m, :, pl.ds(width, width)] = low
                out_ref[m, :, pl.ds(2 * width, width)] = high

    shape = (blocks, width, 3 * width)
    return call(kernel, [(shape, BF), (shape, BF)], [inverse])


def keep(values):
    def kernel(in_ref, out_ref):
        out_ref[...] = in_ref[...]

    return call(kernel, [(values.shape, values.dtype)], [values])[0]


def forward_blocks(tiles, pieces, n_row, n_col, width):
    cols = pieces[0].shape[1]
    depth = tiles.shape[1]
    count = len(pieces)

    def kernel(*refs):
        tile_ref, piece_refs, outs = refs[0], refs[1 : 1 + count], refs[1 + count : -1]
        buf = refs[-1]
        lay_out(piece_refs, buf, n_row, "row")
        emit_blocks(lambda i: dot(tile_ref[rows(i, width), :], buf[...]), outs, n_col, "col")

    outs = block_outs(n_col, width, cols) + [((depth, cols), BF)]
    got = call(kernel, outs, [tiles, *pieces], flops=2 * tiles.shape[0] * depth * cols)
    return got[:-1], got[-1]


def plain_product(tiles, values, transposed):
    cols = values.shape[1]
    product = dot_t if transposed else dot

    def kernel(tile_ref, value_ref, out_ref):
        out_ref[...] = product(tile_ref[...], value_ref[...])

    shape = (tiles.shape[1] if transposed else tiles.shape[0], cols)
    return call(kernel, [(shape, F32)], [tiles, values], flops=2 * tiles.shape[0] * tiles.shape[1] * cols)[0]


def solve_forward(sums, right_side, inverse):
    count = len(sums)

    def kernel(*refs):
        rhs_ref, inv_ref, y_ref, yb_ref = refs[count:]
        y = apply_split(inv_ref[0], rhs_ref[...].astype(F32) - total_of(refs[:count]))
        y_ref[...] = y
        yb_ref[...] = y.astype(BF)

    shape = right_side.shape
    return call(kernel, [(shape, F32), (shape, BF)], [*sums, right_side, inverse])


def top_halves(tiles, pieces, leaf_part, n_row):
    cols = pieces[0].shape[1]
    half = cols // 2
    count = len(pieces)

    def kernel(*refs):
        tile_ref, piece_refs = refs[0], refs[1 : 1 + count]
        part_ref, mine_ref, other_ref, buf = refs[1 + count :]
        lay_out(piece_refs, buf, n_row, "row")
        sec = lax.axis_index("sec")
        for out_ref, which in ((other_ref, 1 - sec), (mine_ref, sec)):
            columns = rows(which, half)
            out = part_ref[:, columns] + dot(tile_ref[...], buf[:, columns])
            out_ref[...] = out.astype(out_ref.dtype)

    shape = (tiles.shape[0], half)
    return call(
        kernel,
        [(shape, F32), (shape, F32)],
        [tiles, *pieces, leaf_part],
        scratch=[((tiles.shape[1], cols), BF)],
        flops=2 * tiles.shape[0] * tiles.shape[1] * cols,
    )


def add_sections(mine, other, n_col, width):
    half = mine.shape[1]

    def kernel(mine_ref, other_ref, *outs):
        emit_blocks(lambda i: mine_ref[rows(i, width), :] + other_ref[rows(i, width), :], outs, n_col, "col")

    return call(kernel, block_outs(n_col, width, half), [mine, other])


def solve_top(sums, right_side, lower, upper):
    count = len(sums)
    half = right_side.shape[1] // 2

    def kernel(*refs):
        rhs_ref, low_ref, up_ref, x_ref, xb_ref = refs[count:]
        mine = rhs_ref[:, rows(lax.axis_index("sec"), half)].astype(F32)
        y = apply_split(low_ref[0], mine - total_of(refs[:count]))
        x = apply_split(up_ref[0], y)
        x_ref[...] = x
        xb_ref[...] = x.astype(BF)

    shape = (right_side.shape[0], half)
    return call(kernel, [(shape, F32), (shape, BF)], [*sums, right_side, lower, upper])


def stack_pieces(pieces, n, axis):
    if not is_direct(n):
        return pieces[0]

    def kernel(*refs):
        lay_out(refs[:-1], refs[-1], n, axis)

    shape = (n * pieces[0].shape[0], pieces[0].shape[1])
    return call(kernel, [(shape, BF)], list(pieces))[0]


def join_halves(mine, other):
    half = mine.shape[1]

    def kernel(mine_ref, other_ref, out_ref):
        sec = lax.axis_index("sec")
        out_ref[:, rows(sec, half)] = mine_ref[...]
        out_ref[:, rows(1 - sec, half)] = other_ref[...]

    return call(kernel, [((mine.shape[0], 2 * half), mine.dtype)], [mine, other])[0]


def top_back_blocks(tiles, mine, other, n_row, width):
    half = mine.shape[1]

    def kernel(tile_ref, mine_ref, other_ref, *outs):
        buf = outs[-1]
        sec = lax.axis_index("sec")
        buf[:, rows(sec, half)] = mine_ref[...]
        buf[:, rows(1 - sec, half)] = other_ref[...]
        emit_blocks(lambda i: dot_t(tile_ref[:, rows(i, width)], buf[...]), outs[:-1], n_row, "row")

    outs = block_outs(n_row, width, 2 * half) + [((mine.shape[0], 2 * half), BF)]
    got = call(kernel, outs, [tiles, mine, other], flops=4 * tiles.shape[0] * tiles.shape[1] * half)
    return got[:-1], got[-1]


def back_blocks(tiles, pieces, top_part, n_row, n_col, span):
    cols = pieces[0].shape[1]
    count = len(pieces)

    def kernel(*refs):
        tile_ref, piece_refs, part_ref = refs[0], refs[1 : 1 + count], refs[1 + count]
        outs, buf = refs[2 + count : -1], refs[-1]
        lay_out(piece_refs, buf, n_col, "col")
        emit_blocks(
            lambda i: part_ref[rows(i, span), :] + dot_t(tile_ref[:, rows(i, span)], buf[...]),
            outs, n_row, "row",
        )

    return call(
        kernel,
        block_outs(n_row, span, cols),
        [tiles, *pieces, top_part],
        scratch=[((tiles.shape[0], cols), BF)],
        flops=2 * tiles.shape[0] * tiles.shape[1] * cols,
    )


def solve_back(sums, right_side, inverse):
    count = len(sums)
    blocks, width = inverse.shape[:2]
    shape = right_side.shape

    def kernel(*refs):
        y_ref, inv_ref, x_ref, xb_ref = refs[count:]
        rest = y_ref[...] - total_of(refs[:count])
        for m in range(blocks):
            x = apply_split(inv_ref[m], rest[m * width : (m + 1) * width])
            x_ref[pl.ds(m * width, width), :] = x
            xb_ref[pl.ds(m * width, width), :] = x.astype(BF)

    return call(kernel, [(shape, F32), (shape, BF)], [*sums, right_side, inverse])


def solve_last(sums, right_side, inverse):
    count = len(sums)
    blocks, width = inverse.shape[:2]

    def kernel(*refs):
        y_ref, inv_ref, x_ref = refs[count:]
        rest = y_ref[...] - total_of(refs[:count])
        for m in range(blocks):
            x_ref[pl.ds(m * width, width), :] = apply_split(inv_ref[m], rest[m * width : (m + 1) * width])

    return call(kernel, [(right_side.shape, F32)], [*sums, right_side, inverse])[0]


def make_body(n_row, n_col):
    def body(leaf_rhs, sep_rhs, top_rhs, leaf_inv, sep_inv, top_inv,
             sep_leaf, top_leaf, top_sep, *masks):
        leaf_count, width, cols = leaf_rhs.shape[2], leaf_rhs.shape[4], leaf_rhs.shape[5]
        span = leaf_count * width

        leaf_y, leaf_yb = leaf_first(leaf_inv[0, 0, :, 0], leaf_rhs[0, 0, :, 0])
        leaf_pieces = gather(leaf_yb, "row", n_row)
        masked = mask_tiles(
            [values.reshape(n_col, width, -1) for values in (sep_leaf, top_leaf, top_sep)],
            [mask.reshape(n_col, 1, -1) for mask in masks],
            width,
        )
        sl, tl, ts = [values.reshape(n_col * width, -1) for values in masked]
        leaf_low, leaf_up = split_inverse(leaf_inv[0, 0, :, 0])
        sep_low, sep_up = split_inverse(sep_inv[0, 0])
        top_low, top_up = split_inverse(top_inv[0])
        blocks, leaf_col = forward_blocks(sl, leaf_pieces, n_row, n_col, width)
        sums = scatter_sum(blocks, "col", n_col)
        leaf_part = plain_product(tl, leaf_col, False)
        sep_y, sep_yb = solve_forward(sums, sep_rhs[0, 0, 0], sep_low)
        mine, other = top_halves(ts, gather(sep_yb, "row", n_row), leaf_part, n_row)
        blocks = add_sections(mine, swap(other, "sec", 2, 1), n_col, width)
        sums = scatter_sum(blocks, "col", n_col)
        top_xh, top_xhb = solve_top(sums, top_rhs[0, 0], top_low, top_up)
        top_stack = stack_pieces(gather(top_xhb, "col", n_col), n_col, "col")
        blocks, top_row = top_back_blocks(ts, top_stack, swap(top_stack, "sec", 2, 1), n_row, width)
        sums = scatter_sum(blocks, "row", n_row)
        top_part = plain_product(tl, top_row, True)
        top_x = join_halves(top_xh, swap(top_xh, "sec", 2, 1))
        sep_x, sep_xb = solve_back(sums, sep_y, sep_up)
        pieces = gather(sep_xb, "col", n_col)
        sums = scatter_sum(back_blocks(sl, pieces, top_part, n_row, n_col, span), "row", n_row)
        leaf_x = solve_last(sums, leaf_y, leaf_up)
        return (
            leaf_x.reshape(1, 1, leaf_count, 1, width, cols),
            keep(sep_x)[None, None, None],
            top_x[None, None],
        )

    return body


def solution(mesh):
    in_specs = (
        P("sec", "row", None, "col", None, None),
        P("sec", "row", "col", None, None),
        P("row", "col", None, None),
        P("sec", "row", None, "col", None, None),
        P("sec", "row", "col", None, None),
        P("row", "col", None, None),
        P("sec", "row", None, None, None, None, "col", None),
        P("sec", "row", None, None, None, None, "col", None),
        P("sec", "row", None, None, None, "col", None),
        P("sec", "row", None, None, None, "col"),
        P("sec", "row", None, None, None, "col"),
        P("sec", "row", None, None, "col"),
    )
    out_specs = (
        P("sec", "row", None, "col", None, None),
        P("sec", "row", "col", None, None),
        P("row", "col", None, None),
    )
    body = make_body(mesh.shape["row"], mesh.shape["col"])
    return jax.shard_map(body, mesh=mesh, in_specs=in_specs, out_specs=out_specs, check_vma=False)
```

```python
import jax
import jax.numpy as jnp
from jax import lax
from jax.experimental import pallas as pl
from jax.experimental.pallas import tpu as pltpu
from jax.sharding import PartitionSpec as P

BF = jnp.bfloat16
F32 = jnp.float32
VMEM = pl.BlockSpec(memory_space=pltpu.VMEM)


def is_direct(n):
    return n in (1, 2, 4)


def swap(values, axis, n, step):
    return lax.ppermute(values, axis, [(i, i ^ step) for i in range(n)])


def swap_cross(values, axis, n, step):
    pairs = [(s * n + i, (1 - s) * n + (i ^ step)) for s in range(2) for i in range(n)]
    return lax.ppermute(values, ("sec", axis), pairs)


def gather(values, axis, n, step_to=swap):
    if is_direct(n):
        return [values] + [step_to(values, axis, n, d) for d in range(1, n)]
    return [lax.all_gather(values, axis, axis=0, tiled=True)]


def scatter_sum(blocks, axis, n, step_to=swap):
    if is_direct(n):
        return [blocks[0]] + [step_to(blocks[d], axis, n, d) for d in range(1, n)]
    return [lax.psum_scatter(blocks[0], axis, scatter_dimension=0, tiled=True)]


def own_half(n_col):
    sec = lax.axis_index("sec")
    return 1 - sec if is_direct(n_col) else sec


def nbytes(shape, dtype):
    size = jnp.dtype(dtype).itemsize
    for extent in shape:
        size *= extent
    return size


def call(kernel, outs, args, scratch=(), flops=0):
    total = sum(nbytes(s, t) for s, t in list(outs) + list(scratch)) + sum(nbytes(a.shape, a.dtype) for a in args)
    return pl.pallas_call(
        kernel,
        out_shape=tuple(jax.ShapeDtypeStruct(s, t) for s, t in outs),
        in_specs=[VMEM] * len(args),
        out_specs=(VMEM,) * len(outs),
        scratch_shapes=[pltpu.VMEM(s, t) for s, t in scratch],
        compiler_params=pltpu.CompilerParams(vmem_limit_bytes=total + (6 << 20)),
        cost_estimate=pl.CostEstimate(flops=flops, bytes_accessed=total, transcendentals=0),
    )(*args)


def place(n, axis):
    if not is_direct(n):
        return lambda d: d
    me = lax.axis_index(axis)
    return lambda d: me ^ d


def rows(index, size):
    return pl.ds(pl.multiple_of(index * size, size), size)


def dot(a, b):
    return jnp.dot(a, b, preferred_element_type=F32)


def dot_t(a, b):
    return lax.dot_general(a, b, (((0,), (0,)), ((), ())), preferred_element_type=F32)


def split(values):
    high = values.astype(BF)
    return high, (values - high.astype(F32)).astype(BF)


def apply_split(parts, right_side):
    high, low = split(right_side)
    return dot(parts, jnp.concatenate([high, high, low], axis=0))


def total_of(refs):
    total = refs[0][...].astype(F32)
    for ref in refs[1:]:
        total = total + ref[...].astype(F32)
    return total


def lay_out(pieces, buf, n, axis):
    if not is_direct(n):
        buf[...] = pieces[0][...]
        return
    at = place(n, axis)
    size = pieces[0].shape[0]
    for d, piece in enumerate(pieces):
        buf[rows(at(d), size), :] = piece[...]


def block_outs(n, size, cols):
    if is_direct(n):
        return [((size, cols), F32)] + [((size, cols), BF)] * (n - 1)
    return [((n * size, cols), F32)]


def emit_blocks(term, outs, n, axis):
    at = place(n, axis)
    if is_direct(n):
        for d in list(range(1, n)) + [0]:
            outs[d][...] = term(at(d)).astype(outs[d].dtype)
    else:
        size = outs[0].shape[0] // n
        for d in range(n):
            outs[0][pl.ds(d * size, size), :] = term(d)


def leaf_first(leaf_inv, leaf_rhs):
    y = jnp.einsum("mab,mbn->man", leaf_inv, leaf_rhs.astype(F32), precision=lax.Precision.HIGHEST)
    y = y.reshape(-1, leaf_rhs.shape[2])
    return y, y.astype(BF)


def mask_tiles(tile_sets, masks, width):
    count = len(masks)
    n_col = masks[0].shape[0]

    def kernel(*refs):
        mask_refs, tile_refs, outs = refs[:count], refs[count : 2 * count], refs[2 * count :]
        for i in range(count):
            for k in range(masks[i].shape[2]):
                weight = jnp.broadcast_to(mask_refs[i][:, :, k : k + 1].astype(F32), (n_col, 1, width)).astype(BF)
                lanes = pl.ds(k * width, width)
                outs[i][:, :, lanes] = tile_refs[i][:, :, lanes] * weight

    return call(kernel, [(t.shape, BF) for t in tile_sets], [*masks, *tile_sets])


def split_inverse(inverse, transposed):
    blocks, width = inverse.shape[:2]

    def kernel(inv_ref, out_ref):
        for m in range(blocks):
            high, low = split(inv_ref[m].T if transposed else inv_ref[m])
            for k, part in enumerate((high, low, high)):
                out_ref[m, :, pl.ds(k * width, width)] = part

    return call(kernel, [((blocks, width, 3 * width), BF)], [inverse])[0]


def keep(values):
    def kernel(in_ref, out_ref):
        out_ref[...] = in_ref[...]

    return call(kernel, [(values.shape, values.dtype)], [values])[0]


def forward_blocks(tiles, pieces, n_row, n_col, width):
    cols = pieces[0].shape[1]
    depth = tiles.shape[1]
    count = len(pieces)

    def kernel(*refs):
        tile_ref, piece_refs, outs = refs[0], refs[1 : 1 + count], refs[1 + count : -1]
        buf = refs[-1]
        lay_out(piece_refs, buf, n_row, "row")
        emit_blocks(lambda i: dot(tile_ref[rows(i, width), :], buf[...]), outs, n_col, "col")

    outs = block_outs(n_col, width, cols) + [((depth, cols), BF)]
    got = call(kernel, outs, [tiles, *pieces], flops=2 * tiles.shape[0] * depth * cols)
    return got[:-1], got[-1]


def plain_product(tiles, values, transposed):
    cols = values.shape[1]
    product = dot_t if transposed else dot

    def kernel(tile_ref, value_ref, out_ref):
        out_ref[...] = product(tile_ref[...], value_ref[...])

    shape = (tiles.shape[1] if transposed else tiles.shape[0], cols)
    return call(kernel, [(shape, F32)], [tiles, values], flops=2 * tiles.shape[0] * tiles.shape[1] * cols)[0]


def solve_forward(sums, right_side, inverse):
    count = len(sums)

    def kernel(*refs):
        rhs_ref, inv_ref, y_ref, yb_ref = refs[count:]
        y = apply_split(inv_ref[0], rhs_ref[...].astype(F32) - total_of(refs[:count]))
        y_ref[...] = y
        yb_ref[...] = y.astype(BF)

    shape = right_side.shape
    return call(kernel, [(shape, F32), (shape, BF)], [*sums, right_side, inverse])


def top_half(tiles, pieces, leaf_part, n_row, n_col, width, passed):
    cols = pieces[0].shape[1]
    half = cols // 2
    count = len(pieces)

    def kernel(*refs):
        tile_ref, piece_refs = refs[0], refs[1 : 1 + count]
        part_ref, out_ref, buf = refs[1 + count :]
        lay_out(piece_refs, buf, n_row, "row")
        sec = lax.axis_index("sec")
        columns = rows(1 - sec if passed else sec, half)
        out_ref[...] = part_ref[:, columns] + dot(tile_ref[...], buf[:, columns])
        if is_direct(n_col):
            own = rows(lax.axis_index("col"), width)
            columns = rows(sec if passed else 1 - sec, half)
            out_ref[own, :] = part_ref[own, columns] + dot(tile_ref[own, :], buf[:, columns])

    return call(
        kernel,
        [((tiles.shape[0], half), F32)],
        [tiles, *pieces, leaf_part],
        scratch=[((tiles.shape[1], cols), BF)],
        flops=tiles.shape[0] * tiles.shape[1] * cols,
    )[0]


def add_sections(mine, other, n_col, width):
    half = mine.shape[1]

    def kernel(mine_ref, other_ref, *outs):
        emit_blocks(lambda i: mine_ref[rows(i, width), :] + other_ref[rows(i, width), :], outs, n_col, "col")

    return call(kernel, block_outs(n_col, width, half), [mine, other])


def solve_top(sums, right_side, lower, upper, n_col):
    count = len(sums)
    half = right_side.shape[1] // 2

    def kernel(*refs):
        rhs_ref, low_ref, up_ref, x_ref, xb_ref = refs[count:]
        mine = rhs_ref[:, rows(own_half(n_col), half)].astype(F32)
        y = apply_split(low_ref[0], mine - total_of(refs[:count]))
        x = apply_split(up_ref[0], y)
        x_ref[...] = x
        xb_ref[...] = x.astype(BF)

    shape = (right_side.shape[0], half)
    return call(kernel, [(shape, F32), (shape, BF)], [*sums, right_side, lower, upper])


def stack_pieces(pieces, n, axis):
    if not is_direct(n):
        return pieces[0]

    def kernel(*refs):
        lay_out(refs[:-1], refs[-1], n, axis)

    shape = (n * pieces[0].shape[0], pieces[0].shape[1])
    return call(kernel, [(shape, BF)], list(pieces))[0]


def join_halves(mine, other, n_col):
    half = mine.shape[1]

    def kernel(mine_ref, other_ref, out_ref):
        own = own_half(n_col)
        out_ref[:, rows(own, half)] = mine_ref[...]
        out_ref[:, rows(1 - own, half)] = other_ref[...]

    return call(kernel, [((mine.shape[0], 2 * half), mine.dtype)], [mine, other])[0]


def top_back_blocks(tiles, mine, other, n_row, n_col, width):
    half = mine.shape[1]

    def kernel(tile_ref, mine_ref, other_ref, *outs):
        buf = outs[-1]
        sec = lax.axis_index("sec")
        buf[:, rows(sec, half)] = mine_ref[...]
        buf[:, rows(1 - sec, half)] = other_ref[...]
        if is_direct(n_col):
            own = rows(lax.axis_index("col"), width)
            buf[own, rows(1 - sec, half)] = mine_ref[own, :]
            buf[own, rows(sec, half)] = other_ref[own, :]
        emit_blocks(lambda i: dot_t(tile_ref[:, rows(i, width)], buf[...]), outs[:-1], n_row, "row")

    outs = block_outs(n_row, width, 2 * half) + [((mine.shape[0], 2 * half), BF)]
    got = call(kernel, outs, [tiles, mine, other], flops=4 * tiles.shape[0] * tiles.shape[1] * half)
    return got[:-1], got[-1]


def back_blocks(tiles, pieces, top_part, n_row, n_col, span):
    cols = pieces[0].shape[1]
    count = len(pieces)

    def kernel(*refs):
        tile_ref, piece_refs, part_ref = refs[0], refs[1 : 1 + count], refs[1 + count]
        outs, buf = refs[2 + count : -1], refs[-1]
        lay_out(piece_refs, buf, n_col, "col")
        emit_blocks(
            lambda i: part_ref[rows(i, span), :] + dot_t(tile_ref[:, rows(i, span)], buf[...]),
            outs, n_row, "row",
        )

    return call(
        kernel,
        block_outs(n_row, span, cols),
        [tiles, *pieces, top_part],
        scratch=[((tiles.shape[0], cols), BF)],
        flops=2 * tiles.shape[0] * tiles.shape[1] * cols,
    )


def solve_back(sums, right_side, inverse):
    count = len(sums)
    blocks, width = inverse.shape[:2]
    shape = right_side.shape

    def kernel(*refs):
        y_ref, inv_ref, x_ref, xb_ref = refs[count:]
        rest = y_ref[...] - total_of(refs[:count])
        for m in range(blocks):
            x = apply_split(inv_ref[m], rest[m * width : (m + 1) * width])
            x_ref[pl.ds(m * width, width), :] = x
            xb_ref[pl.ds(m * width, width), :] = x.astype(BF)

    return call(kernel, [(shape, F32), (shape, BF)], [*sums, right_side, inverse])


def solve_last(sums, right_side, inverse):
    count = len(sums)
    blocks, width = inverse.shape[:2]

    def kernel(*refs):
        y_ref, inv_ref, x_ref = refs[count:]
        rest = y_ref[...] - total_of(refs[:count])
        for m in range(blocks):
            x_ref[pl.ds(m * width, width), :] = apply_split(inv_ref[m], rest[m * width : (m + 1) * width])

    return call(kernel, [(right_side.shape, F32)], [*sums, right_side, inverse])[0]


def make_body(n_row, n_col):
    def body(leaf_rhs, sep_rhs, top_rhs, leaf_inv, sep_inv, top_inv,
             sep_leaf, top_leaf, top_sep, *masks):
        leaf_count, width, cols = leaf_rhs.shape[2], leaf_rhs.shape[4], leaf_rhs.shape[5]
        span = leaf_count * width

        leaf_y, leaf_yb = leaf_first(leaf_inv[0, 0, :, 0], leaf_rhs[0, 0, :, 0])
        leaf_pieces = gather(leaf_yb, "row", n_row)
        masked = mask_tiles(
            [values.reshape(n_col, width, -1) for values in (sep_leaf, top_leaf, top_sep)],
            [mask.reshape(n_col, 1, -1) for mask in masks],
            width,
        )
        sl, tl, ts = [values.reshape(n_col * width, -1) for values in masked]
        blocks, leaf_col = forward_blocks(sl, leaf_pieces, n_row, n_col, width)
        sums = scatter_sum(blocks, "col", n_col)
        leaf_part = plain_product(tl, leaf_col, False)
        sep_y, sep_yb = solve_forward(sums, sep_rhs[0, 0, 0], split_inverse(sep_inv[0, 0], False))
        pieces = gather(sep_yb, "row", n_row)
        passed = swap(top_half(ts, pieces, leaf_part, n_row, n_col, width, True), "sec", 2, 1)
        kept = top_half(ts, pieces, leaf_part, n_row, n_col, width, False)
        blocks = add_sections(kept, passed, n_col, width)
        sums = scatter_sum(blocks, "col", n_col, swap_cross)
        lower, upper = split_inverse(top_inv[0], False), split_inverse(top_inv[0], True)
        top_xh, top_xhb = solve_top(sums, top_rhs[0, 0], lower, upper, n_col)
        top_stack = stack_pieces(gather(top_xhb, "col", n_col, swap_cross), n_col, "col")
        blocks, top_row = top_back_blocks(ts, top_stack, swap(top_stack, "sec", 2, 1), n_row, n_col, width)
        sums = scatter_sum(blocks, "row", n_row)
        top_part = plain_product(tl, top_row, True)
        top_x = join_halves(top_xh, swap(top_xh, "sec", 2, 1), n_col)
        sep_x, sep_xb = solve_back(sums, sep_y, split_inverse(sep_inv[0, 0], True))
        pieces = gather(sep_xb, "col", n_col)
        sums = scatter_sum(back_blocks(sl, pieces, top_part, n_row, n_col, span), "row", n_row)
        leaf_x = solve_last(sums, leaf_y, split_inverse(leaf_inv[0, 0, :, 0], True))
        return (
            leaf_x.reshape(1, 1, leaf_count, 1, width, cols),
            keep(sep_x)[None, None, None],
            top_x[None, None],
        )

    return body


def solution(mesh):
    in_specs = (
        P("sec", "row", None, "col", None, None),
        P("sec", "row", "col", None, None),
        P("row", "col", None, None),
        P("sec", "row", None, "col", None, None),
        P("sec", "row", "col", None, None),
        P("row", "col", None, None),
        P("sec", "row", None, None, None, None, "col", None),
        P("sec", "row", None, None, None, None, "col", None),
        P("sec", "row", None, None, None, "col", None),
        P("sec", "row", None, None, None, "col"),
        P("sec", "row", None, None, None, "col"),
        P("sec", "row", None, None, "col"),
    )
    out_specs = (
        P("sec", "row", None, "col", None, None),
        P("sec", "row", "col", None, None),
        P("row", "col", None, None),
    )
    body = make_body(mesh.shape["row"], mesh.shape["col"])
    return jax.shard_map(body, mesh=mesh, in_specs=in_specs, out_specs=out_specs, check_vma=False)
```

```python
import jax
import jax.numpy as jnp
from jax import lax
from jax.experimental import pallas as pl
from jax.experimental.pallas import tpu as pltpu
from jax.sharding import PartitionSpec as P

BF = jnp.bfloat16
F32 = jnp.float32
VMEM = pl.BlockSpec(memory_space=pltpu.VMEM)


def is_direct(n):
    return n in (1, 2, 4)


def swap(values, axis, n, step):
    return lax.ppermute(values, axis, [(i, i ^ step) for i in range(n)])


def swap_cross(values, axis, n, step):
    pairs = [(s * n + i, (1 - s) * n + (i ^ step)) for s in range(2) for i in range(n)]
    return lax.ppermute(values, ("sec", axis), pairs)


def gather(values, axis, n, step_to=swap):
    if is_direct(n):
        return [values] + [step_to(values, axis, n, d) for d in range(1, n)]
    return [lax.all_gather(values, axis, axis=0, tiled=True)]


def scatter_sum(blocks, axis, n, step_to=swap):
    if is_direct(n):
        return [blocks[0]] + [step_to(blocks[d], axis, n, d) for d in range(1, n)]
    return [lax.psum_scatter(blocks[0], axis, scatter_dimension=0, tiled=True)]


def own_half(n_col):
    sec = lax.axis_index("sec")
    return 1 - sec if is_direct(n_col) else sec


def nbytes(shape, dtype):
    size = jnp.dtype(dtype).itemsize
    for extent in shape:
        size *= extent
    return size


def call(kernel, outs, args, scratch=(), flops=0):
    total = sum(nbytes(s, t) for s, t in list(outs) + list(scratch)) + sum(nbytes(a.shape, a.dtype) for a in args)
    return pl.pallas_call(
        kernel,
        out_shape=tuple(jax.ShapeDtypeStruct(s, t) for s, t in outs),
        in_specs=[VMEM] * len(args),
        out_specs=(VMEM,) * len(outs),
        scratch_shapes=[pltpu.VMEM(s, t) for s, t in scratch],
        compiler_params=pltpu.CompilerParams(vmem_limit_bytes=total + (6 << 20)),
        cost_estimate=pl.CostEstimate(flops=flops, bytes_accessed=total, transcendentals=0),
    )(*args)


def place(n, axis):
    if not is_direct(n):
        return lambda d: d
    me = lax.axis_index(axis)
    return lambda d: me ^ d


def rows(index, size):
    return pl.ds(pl.multiple_of(index * size, size), size)


def dot(a, b):
    return jnp.dot(a, b, preferred_element_type=F32)


def dot_t(a, b):
    return lax.dot_general(a, b, (((0,), (0,)), ((), ())), preferred_element_type=F32)


def split(values):
    high = values.astype(BF)
    return high, (values - high.astype(F32)).astype(BF)


def apply_split(parts, right_side):
    high, low = split(right_side)
    return dot(parts, jnp.concatenate([high, high, low], axis=0))


def total_of(refs):
    total = refs[0][...].astype(F32)
    for ref in refs[1:]:
        total = total + ref[...].astype(F32)
    return total


def lay_out(pieces, buf, n, axis):
    if not is_direct(n):
        buf[...] = pieces[0][...]
        return
    at = place(n, axis)
    size = pieces[0].shape[0]
    for d, piece in enumerate(pieces):
        buf[rows(at(d), size), :] = piece[...]


def block_outs(n, size, cols, own=True):
    if is_direct(n):
        return [((size, cols), F32)] * own + [((size, cols), BF)] * (n - 1)
    return [((n * size, cols), F32)]


def emit_blocks(term, outs, n, axis):
    at = place(n, axis)
    if is_direct(n):
        for d, out_ref in zip(reversed(range(n)), reversed(outs)):
            out_ref[...] = term(at(d)).astype(out_ref.dtype)
    else:
        size = outs[0].shape[0] // n
        for d in range(n):
            outs[0][pl.ds(d * size, size), :] = term(d)


def leaf_first(leaf_inv, leaf_rhs):
    y = jnp.einsum("mab,mbn->man", leaf_inv, leaf_rhs.astype(F32), precision=lax.Precision.HIGHEST)
    y = y.reshape(-1, leaf_rhs.shape[2])
    return y, y.astype(BF)


def mask_tiles(tile_sets, masks, width):
    count = len(masks)
    n_col = masks[0].shape[0]

    def kernel(*refs):
        mask_refs, tile_refs, outs = refs[:count], refs[count : 2 * count], refs[2 * count :]
        for i in range(count):
            for k in range(masks[i].shape[2]):
                weight = jnp.broadcast_to(mask_refs[i][:, :, k : k + 1].astype(F32), (n_col, 1, width)).astype(BF)
                lanes = pl.ds(k * width, width)
                outs[i][:, :, lanes] = tile_refs[i][:, :, lanes] * weight

    return call(kernel, [(t.shape, BF) for t in tile_sets], [*masks, *tile_sets])


def split_inverse(inverse, transposed):
    blocks, width = inverse.shape[:2]

    def kernel(inv_ref, out_ref):
        for m in range(blocks):
            high, low = split(inv_ref[m].T if transposed else inv_ref[m])
            for k, part in enumerate((high, low, high)):
                out_ref[m, :, pl.ds(k * width, width)] = part

    return call(kernel, [((blocks, width, 3 * width), BF)], [inverse])[0]


def keep(values):
    def kernel(in_ref, out_ref):
        out_ref[...] = in_ref[...]

    return call(kernel, [(values.shape, values.dtype)], [values])[0]


def forward_blocks(tiles, pieces, n_row, n_col, width):
    cols = pieces[0].shape[1]
    depth = tiles.shape[1]
    count = len(pieces)

    def kernel(*refs):
        tile_ref, piece_refs, outs = refs[0], refs[1 : 1 + count], refs[1 + count : -1]
        buf = refs[-1]
        lay_out(piece_refs, buf, n_row, "row")
        emit_blocks(lambda i: dot(tile_ref[rows(i, width), :], buf[...]), outs, n_col, "col")

    outs = block_outs(n_col, width, cols, False) + [((depth, cols), BF)]
    got = call(kernel, outs, [tiles, *pieces], flops=2 * tiles.shape[0] * depth * cols)
    return blocks_of(got, n_col)


def blocks_of(got, n):
    return ([None] if is_direct(n) else []) + list(got[:-1]), got[-1]


def own_forward(tiles, values, width):
    def kernel(tile_ref, value_ref, out_ref):
        out_ref[...] = dot(tile_ref[rows(lax.axis_index("col"), width), :], value_ref[...])

    return call(kernel, [((width, values.shape[1]), F32)], [tiles, values], flops=2 * width * values.size)[0]


def own_back(tiles, values, span, part=None):
    args = [tiles, values] + ([] if part is None else [part])

    def kernel(tile_ref, value_ref, *refs):
        own = rows(lax.axis_index("row"), span)
        out = dot_t(tile_ref[:, own], value_ref[...])
        refs[-1][...] = out if part is None else out + refs[0][own, :]

    return call(kernel, [((span, values.shape[1]), F32)], args, flops=2 * span * values.size)[0]


def plain_product(tiles, values, transposed):
    cols = values.shape[1]
    product = dot_t if transposed else dot

    def kernel(tile_ref, value_ref, out_ref):
        out_ref[...] = product(tile_ref[...], value_ref[...])

    shape = (tiles.shape[1] if transposed else tiles.shape[0], cols)
    return call(kernel, [(shape, F32)], [tiles, values], flops=2 * tiles.shape[0] * tiles.shape[1] * cols)[0]


def solve_forward(sums, right_side, inverse):
    total = sums[0].astype(F32)
    for piece in sums[1:]:
        total = total + piece.astype(F32)
    y = jnp.dot(inverse, right_side.astype(F32) - total, precision=lax.Precision.HIGHEST)
    return y, y.astype(BF)


def top_half(tiles, pieces, leaf_part, n_row, n_col, width, passed):
    cols = pieces[0].shape[1]
    half = cols // 2
    count = len(pieces)

    def kernel(*refs):
        tile_ref, piece_refs = refs[0], refs[1 : 1 + count]
        part_ref, out_ref, buf = refs[1 + count :]
        lay_out(piece_refs, buf, n_row, "row")
        sec = lax.axis_index("sec")
        columns = rows(1 - sec if passed else sec, half)
        out_ref[...] = part_ref[:, columns] + dot(tile_ref[...], buf[:, columns])
        if is_direct(n_col):
            own = rows(lax.axis_index("col"), width)
            columns = rows(sec if passed else 1 - sec, half)
            out_ref[own, :] = part_ref[own, columns] + dot(tile_ref[own, :], buf[:, columns])

    return call(
        kernel,
        [((tiles.shape[0], half), F32)],
        [tiles, *pieces, leaf_part],
        scratch=[((tiles.shape[1], cols), BF)],
        flops=tiles.shape[0] * tiles.shape[1] * cols,
    )[0]


def add_sections(mine, other, n_col, width):
    half = mine.shape[1]

    def kernel(mine_ref, other_ref, *outs):
        emit_blocks(lambda i: mine_ref[rows(i, width), :] + other_ref[rows(i, width), :], outs, n_col, "col")

    return call(kernel, block_outs(n_col, width, half), [mine, other])


def solve_top(sums, right_side, lower, upper, n_col):
    count = len(sums)
    half = right_side.shape[1] // 2

    def kernel(*refs):
        rhs_ref, low_ref, up_ref, x_ref, xb_ref = refs[count:]
        mine = rhs_ref[:, rows(own_half(n_col), half)].astype(F32)
        y = apply_split(low_ref[0], mine - total_of(refs[:count]))
        x = apply_split(up_ref[0], y)
        x_ref[...] = x
        xb_ref[...] = x.astype(BF)

    shape = (right_side.shape[0], half)
    return call(kernel, [(shape, F32), (shape, BF)], [*sums, right_side, lower, upper])


def stack_pieces(pieces, n, axis):
    if not is_direct(n):
        return pieces[0]

    def kernel(*refs):
        lay_out(refs[:-1], refs[-1], n, axis)

    shape = (n * pieces[0].shape[0], pieces[0].shape[1])
    return call(kernel, [(shape, BF)], list(pieces))[0]


def join_halves(mine, other, n_col):
    half = mine.shape[1]

    def kernel(mine_ref, other_ref, out_ref):
        own = own_half(n_col)
        out_ref[:, rows(own, half)] = mine_ref[...]
        out_ref[:, rows(1 - own, half)] = other_ref[...]

    return call(kernel, [((mine.shape[0], 2 * half), mine.dtype)], [mine, other])[0]


def top_back_blocks(tiles, mine, other, n_row, n_col, width):
    half = mine.shape[1]

    def kernel(tile_ref, mine_ref, other_ref, *outs):
        buf = outs[-1]
        sec = lax.axis_index("sec")
        buf[:, rows(sec, half)] = mine_ref[...]
        buf[:, rows(1 - sec, half)] = other_ref[...]
        if is_direct(n_col):
            own = rows(lax.axis_index("col"), width)
            buf[own, rows(1 - sec, half)] = mine_ref[own, :]
            buf[own, rows(sec, half)] = other_ref[own, :]
        emit_blocks(lambda i: dot_t(tile_ref[:, rows(i, width)], buf[...]), outs[:-1], n_row, "row")

    outs = block_outs(n_row, width, 2 * half, False) + [((mine.shape[0], 2 * half), BF)]
    got = call(kernel, outs, [tiles, mine, other], flops=4 * tiles.shape[0] * tiles.shape[1] * half)
    return blocks_of(got, n_row)


def back_blocks(tiles, pieces, top_part, n_row, n_col, span):
    cols = pieces[0].shape[1]
    count = len(pieces)

    def kernel(*refs):
        tile_ref, piece_refs, part_ref = refs[0], refs[1 : 1 + count], refs[1 + count]
        outs, buf = refs[2 + count : -1], refs[-1]
        lay_out(piece_refs, buf, n_col, "col")
        emit_blocks(
            lambda i: part_ref[rows(i, span), :] + dot_t(tile_ref[:, rows(i, span)], buf[...]),
            outs, n_row, "row",
        )

    outs = block_outs(n_row, span, cols, False) + [((tiles.shape[0], cols), BF)]
    got = call(kernel, outs, [tiles, *pieces, top_part], flops=2 * tiles.shape[0] * tiles.shape[1] * cols)
    return blocks_of(got, n_row)


def solve_back(sums, right_side, inverse):
    total = sums[0].astype(F32)
    for piece in sums[1:]:
        total = total + piece.astype(F32)
    x = jnp.einsum("ba,bn->an", inverse, right_side - total, precision=lax.Precision.HIGHEST)
    return x, x.astype(BF)


def solve_last(sums, right_side, inverse):
    count = len(sums)
    blocks, width = inverse.shape[:2]

    def kernel(*refs):
        y_ref, inv_ref, x_ref = refs[count:]
        rest = y_ref[...] - total_of(refs[:count])
        for m in range(blocks):
            x_ref[pl.ds(m * width, width), :] = apply_split(inv_ref[m], rest[m * width : (m + 1) * width])

    return call(kernel, [(right_side.shape, F32)], [*sums, right_side, inverse])[0]


def make_body(n_row, n_col):
    def body(leaf_rhs, sep_rhs, top_rhs, leaf_inv, sep_inv, top_inv,
             sep_leaf, top_leaf, top_sep, *masks):
        leaf_count, width, cols = leaf_rhs.shape[2], leaf_rhs.shape[4], leaf_rhs.shape[5]
        span = leaf_count * width

        leaf_y, leaf_yb = leaf_first(leaf_inv[0, 0, :, 0], leaf_rhs[0, 0, :, 0])
        leaf_pieces = gather(leaf_yb, "row", n_row)
        shaped = [mask.reshape(n_col, 1, -1) for mask in masks]
        sl = mask_tiles([sep_leaf.reshape(n_col, width, -1)], shaped[:1], width)[0].reshape(n_col * width, -1)
        blocks, leaf_col = forward_blocks(sl, leaf_pieces, n_row, n_col, width)
        top_leaf, top_sep, leaf_col = lax.optimization_barrier((top_leaf, top_sep, leaf_col))
        sums = scatter_sum(blocks, "col", n_col)
        tops = [values.reshape(n_col, width, -1) for values in (top_leaf, top_sep)]
        tl, ts = [values.reshape(n_col * width, -1) for values in mask_tiles(tops, shaped[1:], width)]
        if is_direct(n_col):
            sums[0] = own_forward(sl, leaf_col, width)
        leaf_part = plain_product(tl, leaf_col, False)
        sums[0], ts, leaf_part = lax.optimization_barrier((sums[0], ts, leaf_part))
        sep_y, sep_yb = solve_forward(sums, sep_rhs[0, 0, 0], sep_inv[0, 0, 0])
        pieces = gather(sep_yb, "row", n_row)
        passed = swap(top_half(ts, pieces, leaf_part, n_row, n_col, width, True), "sec", 2, 1)
        kept = top_half(ts, pieces, leaf_part, n_row, n_col, width, False)
        blocks = add_sections(kept, passed, n_col, width)
        sums = scatter_sum(blocks, "col", n_col, swap_cross)
        lower, upper = split_inverse(top_inv[0], False), split_inverse(top_inv[0], True)
        top_xh, top_xhb = solve_top(sums, top_rhs[0, 0], lower, upper, n_col)
        top_stack = stack_pieces(gather(top_xhb, "col", n_col, swap_cross), n_col, "col")
        blocks, top_row = top_back_blocks(ts, top_stack, swap(top_stack, "sec", 2, 1), n_row, n_col, width)
        sums = scatter_sum(blocks, "row", n_row)
        if is_direct(n_row):
            sums[0] = own_back(ts, top_row, width)
        top_part = plain_product(tl, top_row, True)
        top_x = join_halves(top_xh, swap(top_xh, "sec", 2, 1), n_col)
        sep_x, sep_xb = solve_back(sums, sep_y, sep_inv[0, 0, 0])
        pieces = gather(sep_xb, "col", n_col)
        blocks, sep_row = back_blocks(sl, pieces, top_part, n_row, n_col, span)
        sums = scatter_sum(blocks, "row", n_row)
        if is_direct(n_row):
            sums[0] = own_back(sl, sep_row, span, top_part)
        leaf_x = solve_last(sums, leaf_y, split_inverse(leaf_inv[0, 0, :, 0], True))
        return (
            leaf_x.reshape(1, 1, leaf_count, 1, width, cols),
            keep(sep_x)[None, None, None],
            top_x[None, None],
        )

    return body


def solution(mesh):
    in_specs = (
        P("sec", "row", None, "col", None, None),
        P("sec", "row", "col", None, None),
        P("row", "col", None, None),
        P("sec", "row", None, "col", None, None),
        P("sec", "row", "col", None, None),
        P("row", "col", None, None),
        P("sec", "row", None, None, None, None, "col", None),
        P("sec", "row", None, None, None, None, "col", None),
        P("sec", "row", None, None, None, "col", None),
        P("sec", "row", None, None, None, "col"),
        P("sec", "row", None, None, None, "col"),
        P("sec", "row", None, None, "col"),
    )
    out_specs = (
        P("sec", "row", None, "col", None, None),
        P("sec", "row", "col", None, None),
        P("row", "col", None, None),
    )
    body = make_body(mesh.shape["row"], mesh.shape["col"])
    return jax.shard_map(body, mesh=mesh, in_specs=in_specs, out_specs=out_specs, check_vma=False)
```

```python
import jax
import jax.numpy as jnp
from jax import lax
from jax.experimental import pallas as pl
from jax.experimental.pallas import tpu as pltpu
from jax.sharding import PartitionSpec as P

BF = jnp.bfloat16
F32 = jnp.float32
VMEM = pl.BlockSpec(memory_space=pltpu.VMEM)


def is_direct(n):
    return n in (1, 2, 4)


def steps_of(n):
    return [0] + list(range(n - 1, 0, -1))


def swap(values, axis, n, step):
    return lax.ppermute(values, axis, [(i, i ^ step) for i in range(n)])


def swap_cross(values, axis, n, step):
    pairs = [(s * n + i, (1 - s) * n + (i ^ step)) for s in range(2) for i in range(n)]
    return lax.ppermute(values, ("sec", axis), pairs)


def gather(values, axis, n, step_to=swap):
    if is_direct(n):
        return [values] + [step_to(values, axis, n, d) for d in steps_of(n)[1:]]
    return [lax.all_gather(values, axis, axis=0, tiled=True)]


def scatter_sum(blocks, axis, n, step_to=swap):
    if is_direct(n):
        return [blocks[0]] + [step_to(block, axis, n, d) for block, d in zip(blocks[1:], steps_of(n)[1:])]
    return [lax.psum_scatter(blocks[0], axis, scatter_dimension=0, tiled=True)]


def own_half(n_col):
    sec = lax.axis_index("sec")
    return 1 - sec if is_direct(n_col) else sec


def nbytes(shape, dtype):
    size = jnp.dtype(dtype).itemsize
    for extent in shape:
        size *= extent
    return size


def call(kernel, outs, args, scratch=(), flops=0):
    total = sum(nbytes(s, t) for s, t in list(outs) + list(scratch)) + sum(nbytes(a.shape, a.dtype) for a in args)
    return pl.pallas_call(
        kernel,
        out_shape=tuple(jax.ShapeDtypeStruct(s, t) for s, t in outs),
        in_specs=[VMEM] * len(args),
        out_specs=(VMEM,) * len(outs),
        scratch_shapes=[pltpu.VMEM(s, t) for s, t in scratch],
        compiler_params=pltpu.CompilerParams(vmem_limit_bytes=total + (6 << 20)),
        cost_estimate=pl.CostEstimate(flops=flops, bytes_accessed=total, transcendentals=0),
    )(*args)


def place(n, axis):
    if not is_direct(n):
        return lambda d: d
    me = lax.axis_index(axis)
    return lambda d: me ^ d


def rows(index, size):
    return pl.ds(pl.multiple_of(index * size, size), size)


def dot(a, b):
    return jnp.dot(a, b, preferred_element_type=F32)


def dot_t(a, b):
    return lax.dot_general(a, b, (((0,), (0,)), ((), ())), preferred_element_type=F32)


def split(values):
    high = values.astype(BF)
    return high, (values - high.astype(F32)).astype(BF)


def apply_split(parts, right_side):
    high, low = split(right_side)
    return dot(parts, jnp.concatenate([high, high, low], axis=0))


def total_of(refs):
    total = refs[0][...].astype(F32)
    for ref in refs[1:]:
        total = total + ref[...].astype(F32)
    return total


def lay_out(pieces, buf, n, axis):
    if not is_direct(n):
        buf[...] = pieces[0][...]
        return
    at = place(n, axis)
    size = pieces[0].shape[0]
    for d, piece in zip(steps_of(n), pieces):
        buf[rows(at(d), size), :] = piece[...]


def block_outs(n, size, cols, own=True):
    if is_direct(n):
        return [((size, cols), F32)] * own + [((size, cols), BF)] * (n - 1)
    return [((n * size, cols), F32)]


def emit_blocks(term, outs, n, axis):
    at = place(n, axis)
    if is_direct(n):
        for d, out_ref in zip(reversed(steps_of(n)), reversed(outs)):
            out_ref[...] = term(at(d)).astype(out_ref.dtype)
    else:
        size = outs[0].shape[0] // n
        for d in range(n):
            outs[0][pl.ds(d * size, size), :] = term(d)


def leaf_first(leaf_inv, leaf_rhs):
    y = jnp.einsum("mab,mbn->man", leaf_inv, leaf_rhs.astype(F32), precision=lax.Precision.HIGHEST)
    y = y.reshape(-1, leaf_rhs.shape[2])
    return y, y.astype(BF)


def mask_tiles(tile_sets, masks, width):
    count = len(masks)
    n_col = masks[0].shape[0]

    def kernel(*refs):
        mask_refs, tile_refs, outs = refs[:count], refs[count : 2 * count], refs[2 * count :]
        for i in range(count):
            for k in range(masks[i].shape[2]):
                weight = jnp.broadcast_to(mask_refs[i][:, :, k : k + 1].astype(F32), (n_col, 1, width)).astype(BF)
                lanes = pl.ds(k * width, width)
                outs[i][:, :, lanes] = tile_refs[i][:, :, lanes] * weight

    return call(kernel, [(t.shape, BF) for t in tile_sets], [*masks, *tile_sets])


def split_inverse(inverse, transposed):
    blocks, width = inverse.shape[:2]

    def kernel(inv_ref, out_ref):
        for m in range(blocks):
            high, low = split(inv_ref[m].T if transposed else inv_ref[m])
            for k, part in enumerate((high, low, high)):
                out_ref[m, :, pl.ds(k * width, width)] = part

    return call(kernel, [((blocks, width, 3 * width), BF)], [inverse])[0]


def keep(values):
    def kernel(in_ref, out_ref):
        out_ref[...] = in_ref[...]

    return call(kernel, [(values.shape, values.dtype)], [values])[0]


def forward_blocks(tiles, pieces, n_row, n_col, width):
    cols = pieces[0].shape[1]
    depth = tiles.shape[1]
    count = len(pieces)

    def kernel(*refs):
        tile_ref, piece_refs, outs = refs[0], refs[1 : 1 + count], refs[1 + count : -1]
        buf = refs[-1]
        lay_out(piece_refs, buf, n_row, "row")
        emit_blocks(lambda i: dot(tile_ref[rows(i, width), :], buf[...]), outs, n_col, "col")

    outs = block_outs(n_col, width, cols, False) + [((depth, cols), BF)]
    got = call(kernel, outs, [tiles, *pieces], flops=2 * tiles.shape[0] * depth * cols)
    return blocks_of(got, n_col)


def blocks_of(got, n):
    return ([None] if is_direct(n) else []) + list(got[:-1]), got[-1]


def own_forward(tiles, values, width):
    def kernel(tile_ref, value_ref, out_ref):
        out_ref[...] = dot(tile_ref[rows(lax.axis_index("col"), width), :], value_ref[...])

    return call(kernel, [((width, values.shape[1]), F32)], [tiles, values], flops=2 * width * values.size)[0]


def own_back(tiles, values, span, part=None):
    args = [tiles, values] + ([] if part is None else [part])

    def kernel(tile_ref, value_ref, *refs):
        own = rows(lax.axis_index("row"), span)
        out = dot_t(tile_ref[:, own], value_ref[...])
        refs[-1][...] = out if part is None else out + refs[0][own, :]

    return call(kernel, [((span, values.shape[1]), F32)], args, flops=2 * span * values.size)[0]


def plain_product(tiles, values, transposed):
    cols = values.shape[1]
    product = dot_t if transposed else dot

    def kernel(tile_ref, value_ref, out_ref):
        out_ref[...] = product(tile_ref[...], value_ref[...])

    shape = (tiles.shape[1] if transposed else tiles.shape[0], cols)
    return call(kernel, [(shape, F32)], [tiles, values], flops=2 * tiles.shape[0] * tiles.shape[1] * cols)[0]


def solve_forward(sums, right_side, inverse):
    total = sums[0].astype(F32)
    for piece in sums[1:]:
        total = total + piece.astype(F32)
    y = jnp.dot(inverse, right_side.astype(F32) - total, precision=lax.Precision.HIGHEST)
    return y, y.astype(BF)


def top_half(tiles, pieces, leaf_part, n_row, n_col, width, passed):
    cols = pieces[0].shape[1]
    half = cols // 2
    count = len(pieces)

    def kernel(*refs):
        tile_ref, piece_refs = refs[0], refs[1 : 1 + count]
        part_ref, out_ref, buf = refs[1 + count :]
        lay_out(piece_refs, buf, n_row, "row")
        sec = lax.axis_index("sec")
        columns = rows(1 - sec if passed else sec, half)
        out_ref[...] = part_ref[:, columns] + dot(tile_ref[...], buf[:, columns])
        if is_direct(n_col):
            own = rows(lax.axis_index("col"), width)
            columns = rows(sec if passed else 1 - sec, half)
            out_ref[own, :] = part_ref[own, columns] + dot(tile_ref[own, :], buf[:, columns])

    return call(
        kernel,
        [((tiles.shape[0], half), F32)],
        [tiles, *pieces, leaf_part],
        scratch=[((tiles.shape[1], cols), BF)],
        flops=tiles.shape[0] * tiles.shape[1] * cols,
    )[0]


def add_sections(mine, other, n_col, width):
    half = mine.shape[1]

    def kernel(mine_ref, other_ref, *outs):
        emit_blocks(lambda i: mine_ref[rows(i, width), :] + other_ref[rows(i, width), :], outs, n_col, "col")

    return call(kernel, block_outs(n_col, width, half), [mine, other])


def solve_top(sums, right_side, lower, upper, n_col):
    count = len(sums)
    half = right_side.shape[1] // 2

    def kernel(*refs):
        rhs_ref, low_ref, up_ref, x_ref, xb_ref = refs[count:]
        mine = rhs_ref[:, rows(own_half(n_col), half)].astype(F32)
        y = apply_split(low_ref[0], mine - total_of(refs[:count]))
        x = apply_split(up_ref[0], y)
        x_ref[...] = x
        xb_ref[...] = x.astype(BF)

    shape = (right_side.shape[0], half)
    return call(kernel, [(shape, F32), (shape, BF)], [*sums, right_side, lower, upper])


def stack_pieces(pieces, n, axis):
    if not is_direct(n):
        return pieces[0]

    def kernel(*refs):
        lay_out(refs[:-1], refs[-1], n, axis)

    shape = (n * pieces[0].shape[0], pieces[0].shape[1])
    return call(kernel, [(shape, BF)], list(pieces))[0]


def join_halves(mine, other, n_col):
    half = mine.shape[1]

    def kernel(mine_ref, other_ref, out_ref):
        own = own_half(n_col)
        out_ref[:, rows(own, half)] = mine_ref[...]
        out_ref[:, rows(1 - own, half)] = other_ref[...]

    return call(kernel, [((mine.shape[0], 2 * half), mine.dtype)], [mine, other])[0]


def top_back_blocks(tiles, mine, other, n_row, n_col, width):
    half = mine.shape[1]

    def kernel(tile_ref, mine_ref, other_ref, *outs):
        buf = outs[-1]
        sec = lax.axis_index("sec")
        buf[:, rows(sec, half)] = mine_ref[...]
        buf[:, rows(1 - sec, half)] = other_ref[...]
        if is_direct(n_col):
            own = rows(lax.axis_index("col"), width)
            buf[own, rows(1 - sec, half)] = mine_ref[own, :]
            buf[own, rows(sec, half)] = other_ref[own, :]
        emit_blocks(lambda i: dot_t(tile_ref[:, rows(i, width)], buf[...]), outs[:-1], n_row, "row")

    outs = block_outs(n_row, width, 2 * half, False) + [((mine.shape[0], 2 * half), BF)]
    got = call(kernel, outs, [tiles, mine, other], flops=4 * tiles.shape[0] * tiles.shape[1] * half)
    return blocks_of(got, n_row)


def back_blocks(tiles, pieces, top_part, n_row, n_col, span):
    cols = pieces[0].shape[1]
    count = len(pieces)

    def kernel(*refs):
        tile_ref, piece_refs, part_ref = refs[0], refs[1 : 1 + count], refs[1 + count]
        outs, buf = refs[2 + count : -1], refs[-1]
        lay_out(piece_refs, buf, n_col, "col")
        emit_blocks(
            lambda i: part_ref[rows(i, span), :] + dot_t(tile_ref[:, rows(i, span)], buf[...]),
            outs, n_row, "row",
        )

    outs = block_outs(n_row, span, cols, False) + [((tiles.shape[0], cols), BF)]
    got = call(kernel, outs, [tiles, *pieces, top_part], flops=2 * tiles.shape[0] * tiles.shape[1] * cols)
    return blocks_of(got, n_row)


def solve_back(sums, right_side, inverse):
    total = sums[0].astype(F32)
    for piece in sums[1:]:
        total = total + piece.astype(F32)
    x = jnp.einsum("ba,bn->an", inverse, right_side - total, precision=lax.Precision.HIGHEST)
    return x, x.astype(BF)


def solve_last(sums, right_side, inverse):
    count = len(sums)
    blocks, width = inverse.shape[:2]

    def kernel(*refs):
        y_ref, inv_ref, x_ref = refs[count:]
        rest = y_ref[...] - total_of(refs[:count])
        for m in range(blocks):
            x_ref[pl.ds(m * width, width), :] = apply_split(inv_ref[m], rest[m * width : (m + 1) * width])

    return call(kernel, [(right_side.shape, F32)], [*sums, right_side, inverse])[0]


def make_body(n_row, n_col):
    def body(leaf_rhs, sep_rhs, top_rhs, leaf_inv, sep_inv, top_inv,
             sep_leaf, top_leaf, top_sep, *masks):
        leaf_count, width, cols = leaf_rhs.shape[2], leaf_rhs.shape[4], leaf_rhs.shape[5]
        span = leaf_count * width

        leaf_y, leaf_yb = leaf_first(leaf_inv[0, 0, :, 0], leaf_rhs[0, 0, :, 0])
        leaf_pieces = gather(leaf_yb, "row", n_row)
        shaped = [mask.reshape(n_col, 1, -1) for mask in masks]
        sl = mask_tiles([sep_leaf.reshape(n_col, width, -1)], shaped[:1], width)[0].reshape(n_col * width, -1)
        blocks, leaf_col = forward_blocks(sl, leaf_pieces, n_row, n_col, width)
        top_leaf, top_sep, leaf_col = lax.optimization_barrier((top_leaf, top_sep, leaf_col))
        sums = scatter_sum(blocks, "col", n_col)
        tops = [values.reshape(n_col, width, -1) for values in (top_leaf, top_sep)]
        tl, ts = [values.reshape(n_col * width, -1) for values in mask_tiles(tops, shaped[1:], width)]
        if is_direct(n_col):
            sums[0] = own_forward(sl, leaf_col, width)
        leaf_part = plain_product(tl, leaf_col, False)
        sums[0], ts, leaf_part = lax.optimization_barrier((sums[0], ts, leaf_part))
        sep_y, sep_yb = solve_forward(sums, sep_rhs[0, 0, 0], sep_inv[0, 0, 0])
        pieces = gather(sep_yb, "row", n_row)
        passed = swap(top_half(ts, pieces, leaf_part, n_row, n_col, width, True), "sec", 2, 1)
        kept = top_half(ts, pieces, leaf_part, n_row, n_col, width, False)
        blocks = add_sections(kept, passed, n_col, width)
        sums = scatter_sum(blocks, "col", n_col, swap_cross)
        lower, upper = split_inverse(top_inv[0], False), split_inverse(top_inv[0], True)
        top_xh, top_xhb = solve_top(sums, top_rhs[0, 0], lower, upper, n_col)
        top_stack = stack_pieces(gather(top_xhb, "col", n_col, swap_cross), n_col, "col")
        blocks, top_row = top_back_blocks(ts, top_stack, swap(top_stack, "sec", 2, 1), n_row, n_col, width)
        sums = scatter_sum(blocks, "row", n_row)
        if is_direct(n_row):
            sums[0] = own_back(ts, top_row, width)
        top_part = plain_product(tl, top_row, True)
        top_x = join_halves(top_xh, swap(top_xh, "sec", 2, 1), n_col)
        sep_x, sep_xb = solve_back(sums, sep_y, sep_inv[0, 0, 0])
        pieces = gather(sep_xb, "col", n_col)
        blocks, sep_row = back_blocks(sl, pieces, top_part, n_row, n_col, span)
        sums = scatter_sum(blocks, "row", n_row)
        if is_direct(n_row):
            sums[0] = own_back(sl, sep_row, span, top_part)
        leaf_x = solve_last(sums, leaf_y, split_inverse(leaf_inv[0, 0, :, 0], True))
        return (
            leaf_x.reshape(1, 1, leaf_count, 1, width, cols),
            keep(sep_x)[None, None, None],
            top_x[None, None],
        )

    return body


def solution(mesh):
    in_specs = (
        P("sec", "row", None, "col", None, None),
        P("sec", "row", "col", None, None),
        P("row", "col", None, None),
        P("sec", "row", None, "col", None, None),
        P("sec", "row", "col", None, None),
        P("row", "col", None, None),
        P("sec", "row", None, None, None, None, "col", None),
        P("sec", "row", None, None, None, None, "col", None),
        P("sec", "row", None, None, None, "col", None),
        P("sec", "row", None, None, None, "col"),
        P("sec", "row", None, None, None, "col"),
        P("sec", "row", None, None, "col"),
    )
    out_specs = (
        P("sec", "row", None, "col", None, None),
        P("sec", "row", "col", None, None),
        P("row", "col", None, None),
    )
    body = make_body(mesh.shape["row"], mesh.shape["col"])
    return jax.shard_map(body, mesh=mesh, in_specs=in_specs, out_specs=out_specs, check_vma=False)
```

```python
import jax
import jax.numpy as jnp
from jax import lax
from jax.experimental import pallas as pl
from jax.experimental.pallas import tpu as pltpu
from jax.sharding import PartitionSpec as P

BF = jnp.bfloat16
F32 = jnp.float32
VMEM = pl.BlockSpec(memory_space=pltpu.VMEM)


def is_direct(n):
    return n in (1, 2, 4)


ORDERS = {"row": (3, 1, 2), "col": (2, 3, 1), "cross": (2, 3, 1)}


def steps_of(n, kind):
    return [0] + [d for d in ORDERS[kind] if d < n]


def swap(values, axis, n, step):
    return lax.ppermute(values, axis, [(i, i ^ step) for i in range(n)])


def swap_cross(values, axis, n, step):
    pairs = [(s * n + i, (1 - s) * n + (i ^ step)) for s in range(2) for i in range(n)]
    return lax.ppermute(values, ("sec", axis), pairs)


def kind_of(step_to, axis):
    return "cross" if step_to is swap_cross else axis


def gather(values, axis, n, step_to=swap):
    if is_direct(n):
        return [values] + [step_to(values, axis, n, d) for d in steps_of(n, kind_of(step_to, axis))[1:]]
    return [lax.all_gather(values, axis, axis=0, tiled=True)]


def scatter_sum(blocks, axis, n, step_to=swap):
    if is_direct(n):
        return [blocks[0]] + [step_to(block, axis, n, d) for block, d in zip(blocks[1:], steps_of(n, kind_of(step_to, axis))[1:])]
    return [lax.psum_scatter(blocks[0], axis, scatter_dimension=0, tiled=True)]


def own_half(n_col):
    sec = lax.axis_index("sec")
    return 1 - sec if is_direct(n_col) else sec


def nbytes(shape, dtype):
    size = jnp.dtype(dtype).itemsize
    for extent in shape:
        size *= extent
    return size


def call(kernel, outs, args, scratch=(), flops=0):
    total = sum(nbytes(s, t) for s, t in list(outs) + list(scratch)) + sum(nbytes(a.shape, a.dtype) for a in args)
    return pl.pallas_call(
        kernel,
        out_shape=tuple(jax.ShapeDtypeStruct(s, t) for s, t in outs),
        in_specs=[VMEM] * len(args),
        out_specs=(VMEM,) * len(outs),
        scratch_shapes=[pltpu.VMEM(s, t) for s, t in scratch],
        compiler_params=pltpu.CompilerParams(vmem_limit_bytes=total + (6 << 20)),
        cost_estimate=pl.CostEstimate(flops=flops, bytes_accessed=total, transcendentals=0),
    )(*args)


def place(n, axis):
    if not is_direct(n):
        return lambda d: d
    me = lax.axis_index(axis)
    return lambda d: me ^ d


def rows(index, size):
    return pl.ds(pl.multiple_of(index * size, size), size)


def dot(a, b):
    return jnp.dot(a, b, preferred_element_type=F32)


def dot_t(a, b):
    return lax.dot_general(a, b, (((0,), (0,)), ((), ())), preferred_element_type=F32)


def split(values):
    high = values.astype(BF)
    return high, (values - high.astype(F32)).astype(BF)


def apply_split(parts, right_side):
    high, low = split(right_side)
    return dot(parts, jnp.concatenate([high, high, low], axis=0))


def total_of(refs):
    total = refs[0][...].astype(F32)
    for ref in refs[1:]:
        total = total + ref[...].astype(F32)
    return total


def lay_out(pieces, buf, n, axis, kind=None):
    if not is_direct(n):
        buf[...] = pieces[0][...]
        return
    at = place(n, axis)
    size = pieces[0].shape[0]
    for d, piece in zip(steps_of(n, kind or axis), pieces):
        buf[rows(at(d), size), :] = piece[...]


def block_outs(n, size, cols, own=True):
    if is_direct(n):
        return [((size, cols), F32)] * own + [((size, cols), BF)] * (n - 1)
    return [((n * size, cols), F32)]


def emit_blocks(term, outs, n, axis, kind=None):
    at = place(n, axis)
    if is_direct(n):
        for d, out_ref in zip(reversed(steps_of(n, kind or axis)), reversed(outs)):
            out_ref[...] = term(at(d)).astype(out_ref.dtype)
    else:
        size = outs[0].shape[0] // n
        for d in range(n):
            outs[0][pl.ds(d * size, size), :] = term(d)


def leaf_first(leaf_inv, leaf_rhs):
    y = jnp.einsum("mab,mbn->man", leaf_inv, leaf_rhs.astype(F32), precision=lax.Precision.HIGHEST)
    y = y.reshape(-1, leaf_rhs.shape[2])
    return y, y.astype(BF)


def mask_tiles(tile_sets, masks, width):
    count = len(masks)
    n_col = masks[0].shape[0]

    def kernel(*refs):
        mask_refs, tile_refs, outs = refs[:count], refs[count : 2 * count], refs[2 * count :]
        for i in range(count):
            for k in range(masks[i].shape[2]):
                weight = jnp.broadcast_to(mask_refs[i][:, :, k : k + 1].astype(F32), (n_col, 1, width)).astype(BF)
                lanes = pl.ds(k * width, width)
                outs[i][:, :, lanes] = tile_refs[i][:, :, lanes] * weight

    return call(kernel, [(t.shape, BF) for t in tile_sets], [*masks, *tile_sets])


def split_inverse(inverse, transposed):
    blocks, width = inverse.shape[:2]

    def kernel(inv_ref, out_ref):
        for m in range(blocks):
            high, low = split(inv_ref[m].T if transposed else inv_ref[m])
            for k, part in enumerate((high, low, high)):
                out_ref[m, :, pl.ds(k * width, width)] = part

    return call(kernel, [((blocks, width, 3 * width), BF)], [inverse])[0]


def keep(values):
    def kernel(in_ref, out_ref):
        out_ref[...] = in_ref[...]

    return call(kernel, [(values.shape, values.dtype)], [values])[0]


def forward_blocks(tiles, pieces, n_row, n_col, width):
    cols = pieces[0].shape[1]
    depth = tiles.shape[1]
    count = len(pieces)

    def kernel(*refs):
        tile_ref, piece_refs, outs = refs[0], refs[1 : 1 + count], refs[1 + count : -1]
        buf = refs[-1]
        lay_out(piece_refs, buf, n_row, "row")
        emit_blocks(lambda i: dot(tile_ref[rows(i, width), :], buf[...]), outs, n_col, "col")

    outs = block_outs(n_col, width, cols, False) + [((depth, cols), BF)]
    got = call(kernel, outs, [tiles, *pieces], flops=2 * tiles.shape[0] * depth * cols)
    return blocks_of(got, n_col)


def blocks_of(got, n):
    return ([None] if is_direct(n) else []) + list(got[:-1]), got[-1]


def own_forward(tiles, values, width):
    def kernel(tile_ref, value_ref, out_ref):
        out_ref[...] = dot(tile_ref[rows(lax.axis_index("col"), width), :], value_ref[...])

    return call(kernel, [((width, values.shape[1]), F32)], [tiles, values], flops=2 * width * values.size)[0]


def own_back(tiles, values, span, part=None):
    args = [tiles, values] + ([] if part is None else [part])

    def kernel(tile_ref, value_ref, *refs):
        own = rows(lax.axis_index("row"), span)
        out = dot_t(tile_ref[:, own], value_ref[...])
        refs[-1][...] = out if part is None else out + refs[0][own, :]

    return call(kernel, [((span, values.shape[1]), F32)], args, flops=2 * span * values.size)[0]


def plain_product(tiles, values, transposed):
    cols = values.shape[1]
    product = dot_t if transposed else dot

    def kernel(tile_ref, value_ref, out_ref):
        out_ref[...] = product(tile_ref[...], value_ref[...])

    shape = (tiles.shape[1] if transposed else tiles.shape[0], cols)
    return call(kernel, [(shape, F32)], [tiles, values], flops=2 * tiles.shape[0] * tiles.shape[1] * cols)[0]


def solve_forward(sums, right_side, inverse):
    total = sums[0].astype(F32)
    for piece in sums[1:]:
        total = total + piece.astype(F32)
    y = jnp.dot(inverse, right_side.astype(F32) - total, precision=lax.Precision.HIGHEST)
    return y, y.astype(BF)


def top_half(tiles, pieces, leaf_part, n_row, n_col, width, passed):
    cols = pieces[0].shape[1]
    half = cols // 2
    count = len(pieces)

    def kernel(*refs):
        tile_ref, piece_refs = refs[0], refs[1 : 1 + count]
        part_ref, out_ref, buf = refs[1 + count :]
        lay_out(piece_refs, buf, n_row, "row")
        sec = lax.axis_index("sec")
        columns = rows(1 - sec if passed else sec, half)
        out_ref[...] = part_ref[:, columns] + dot(tile_ref[...], buf[:, columns])
        if is_direct(n_col):
            own = rows(lax.axis_index("col"), width)
            columns = rows(sec if passed else 1 - sec, half)
            out_ref[own, :] = part_ref[own, columns] + dot(tile_ref[own, :], buf[:, columns])

    return call(
        kernel,
        [((tiles.shape[0], half), F32)],
        [tiles, *pieces, leaf_part],
        scratch=[((tiles.shape[1], cols), BF)],
        flops=tiles.shape[0] * tiles.shape[1] * cols,
    )[0]


def add_sections(mine, other, n_col, width):
    half = mine.shape[1]

    def kernel(mine_ref, other_ref, *outs):
        emit_blocks(lambda i: mine_ref[rows(i, width), :] + other_ref[rows(i, width), :], outs, n_col, "col", "cross")

    return call(kernel, block_outs(n_col, width, half), [mine, other])


def square_inverse(inverse):
    width = inverse.shape[1]

    def kernel(inv_ref, out_ref):
        value = inv_ref[0]
        full = lax.dot_general(value, value, (((0,), (0,)), ((), ())), precision=lax.Precision.HIGHEST, preferred_element_type=F32)
        high, low = split(full)
        for k, part in enumerate((high, low, high)):
            out_ref[:, pl.ds(k * width, width)] = part

    return call(kernel, [((width, 3 * width), BF)], [inverse])[0]


def solve_top(sums, right_side, square, n_col):
    count = len(sums)
    half = right_side.shape[1] // 2

    def kernel(*refs):
        rhs_ref, sq_ref, x_ref, xb_ref = refs[count:]
        mine = rhs_ref[:, rows(own_half(n_col), half)].astype(F32)
        x = apply_split(sq_ref[...], mine - total_of(refs[:count]))
        x_ref[...] = x
        xb_ref[...] = x.astype(BF)

    shape = (right_side.shape[0], half)
    return call(kernel, [(shape, F32), (shape, BF)], [*sums, right_side, square])


def stack_pieces(pieces, n, axis):
    if not is_direct(n):
        return pieces[0]

    def kernel(*refs):
        lay_out(refs[:-1], refs[-1], n, axis, "cross")

    shape = (n * pieces[0].shape[0], pieces[0].shape[1])
    return call(kernel, [(shape, BF)], list(pieces))[0]


def join_halves(mine, other, n_col):
    half = mine.shape[1]

    def kernel(mine_ref, other_ref, out_ref):
        own = own_half(n_col)
        out_ref[:, rows(own, half)] = mine_ref[...]
        out_ref[:, rows(1 - own, half)] = other_ref[...]

    return call(kernel, [((mine.shape[0], 2 * half), mine.dtype)], [mine, other])[0]


def top_back_blocks(tiles, mine, other, n_row, n_col, width):
    half = mine.shape[1]

    def kernel(tile_ref, mine_ref, other_ref, *outs):
        buf = outs[-1]
        sec = lax.axis_index("sec")
        buf[:, rows(sec, half)] = mine_ref[...]
        buf[:, rows(1 - sec, half)] = other_ref[...]
        if is_direct(n_col):
            own = rows(lax.axis_index("col"), width)
            buf[own, rows(1 - sec, half)] = mine_ref[own, :]
            buf[own, rows(sec, half)] = other_ref[own, :]
        emit_blocks(lambda i: dot_t(tile_ref[:, rows(i, width)], buf[...]), outs[:-1], n_row, "row")

    outs = block_outs(n_row, width, 2 * half, False) + [((mine.shape[0], 2 * half), BF)]
    got = call(kernel, outs, [tiles, mine, other], flops=4 * tiles.shape[0] * tiles.shape[1] * half)
    return blocks_of(got, n_row)


def back_blocks(tiles, pieces, top_part, n_row, n_col, span):
    cols = pieces[0].shape[1]
    count = len(pieces)

    def kernel(*refs):
        tile_ref, piece_refs, part_ref = refs[0], refs[1 : 1 + count], refs[1 + count]
        outs, buf = refs[2 + count : -1], refs[-1]
        lay_out(piece_refs, buf, n_col, "col")
        emit_blocks(
            lambda i: part_ref[rows(i, span), :] + dot_t(tile_ref[:, rows(i, span)], buf[...]),
            outs, n_row, "row",
        )

    outs = block_outs(n_row, span, cols, False) + [((tiles.shape[0], cols), BF)]
    got = call(kernel, outs, [tiles, *pieces, top_part], flops=2 * tiles.shape[0] * tiles.shape[1] * cols)
    return blocks_of(got, n_row)


def solve_back(sums, right_side, inverse):
    total = sums[0].astype(F32)
    for piece in sums[1:]:
        total = total + piece.astype(F32)
    x = jnp.einsum("ba,bn->an", inverse, right_side - total, precision=lax.Precision.HIGHEST)
    return x, x.astype(BF)


def solve_last(sums, right_side, inverse):
    count = len(sums)
    blocks, width = inverse.shape[:2]

    def kernel(*refs):
        y_ref, inv_ref, x_ref = refs[count:]
        rest = y_ref[...] - total_of(refs[:count])
        for m in range(blocks):
            x_ref[pl.ds(m * width, width), :] = apply_split(inv_ref[m], rest[m * width : (m + 1) * width])

    return call(kernel, [(right_side.shape, F32)], [*sums, right_side, inverse])[0]


def make_body(n_row, n_col):
    def body(leaf_rhs, sep_rhs, top_rhs, leaf_inv, sep_inv, top_inv,
             sep_leaf, top_leaf, top_sep, *masks):
        leaf_count, width, cols = leaf_rhs.shape[2], leaf_rhs.shape[4], leaf_rhs.shape[5]
        span = leaf_count * width

        leaf_y, leaf_yb = leaf_first(leaf_inv[0, 0, :, 0], leaf_rhs[0, 0, :, 0])
        leaf_pieces = gather(leaf_yb, "row", n_row)
        shaped = [mask.reshape(n_col, 1, -1) for mask in masks]
        sl = mask_tiles([sep_leaf.reshape(n_col, width, -1)], shaped[:1], width)[0].reshape(n_col * width, -1)
        blocks, leaf_col = forward_blocks(sl, leaf_pieces, n_row, n_col, width)
        top_leaf, top_sep, leaf_col = lax.optimization_barrier((top_leaf, top_sep, leaf_col))
        sums = scatter_sum(blocks, "col", n_col)
        tops = [values.reshape(n_col, width, -1) for values in (top_leaf, top_sep)]
        tl, ts = [values.reshape(n_col * width, -1) for values in mask_tiles(tops, shaped[1:], width)]
        if is_direct(n_col):
            sums[0] = own_forward(sl, leaf_col, width)
        leaf_part = plain_product(tl, leaf_col, False)
        sums[0], ts, leaf_part = lax.optimization_barrier((sums[0], ts, leaf_part))
        sep_y, sep_yb = solve_forward(sums, sep_rhs[0, 0, 0], sep_inv[0, 0, 0])
        pieces = gather(sep_yb, "row", n_row)
        passed = swap(top_half(ts, pieces, leaf_part, n_row, n_col, width, True), "sec", 2, 1)
        kept = top_half(ts, pieces, leaf_part, n_row, n_col, width, False)
        blocks = add_sections(kept, passed, n_col, width)
        sums = scatter_sum(blocks, "col", n_col, swap_cross)
        top_xh, top_xhb = solve_top(sums, top_rhs[0, 0], square_inverse(top_inv[0]), n_col)
        top_stack = stack_pieces(gather(top_xhb, "col", n_col, swap_cross), n_col, "col")
        blocks, top_row = top_back_blocks(ts, top_stack, swap(top_stack, "sec", 2, 1), n_row, n_col, width)
        sums = scatter_sum(blocks, "row", n_row)
        if is_direct(n_row):
            sums[0] = own_back(ts, top_row, width)
        top_part = plain_product(tl, top_row, True)
        top_x = join_halves(top_xh, swap(top_xh, "sec", 2, 1), n_col)
        sep_x, sep_xb = solve_back(sums, sep_y, sep_inv[0, 0, 0])
        pieces = gather(sep_xb, "col", n_col)
        blocks, sep_row = back_blocks(sl, pieces, top_part, n_row, n_col, span)
        sums = scatter_sum(blocks, "row", n_row)
        if is_direct(n_row):
            sums[0] = own_back(sl, sep_row, span, top_part)
        leaf_x = solve_last(sums, leaf_y, split_inverse(leaf_inv[0, 0, :, 0], True))
        return (
            leaf_x.reshape(1, 1, leaf_count, 1, width, cols),
            keep(sep_x)[None, None, None],
            top_x[None, None],
        )

    return body


def solution(mesh):
    in_specs = (
        P("sec", "row", None, "col", None, None),
        P("sec", "row", "col", None, None),
        P("row", "col", None, None),
        P("sec", "row", None, "col", None, None),
        P("sec", "row", "col", None, None),
        P("row", "col", None, None),
        P("sec", "row", None, None, None, None, "col", None),
        P("sec", "row", None, None, None, None, "col", None),
        P("sec", "row", None, None, None, "col", None),
        P("sec", "row", None, None, None, "col"),
        P("sec", "row", None, None, None, "col"),
        P("sec", "row", None, None, "col"),
    )
    out_specs = (
        P("sec", "row", None, "col", None, None),
        P("sec", "row", "col", None, None),
        P("row", "col", None, None),
    )
    body = make_body(mesh.shape["row"], mesh.shape["col"])
    return jax.shard_map(body, mesh=mesh, in_specs=in_specs, out_specs=out_specs, check_vma=False)
```

```python
import jax
import jax.numpy as jnp
from jax import lax
from jax.experimental import pallas as pl
from jax.experimental.pallas import tpu as pltpu
from jax.sharding import PartitionSpec as P

BF = jnp.bfloat16
F32 = jnp.float32
VMEM = pl.BlockSpec(memory_space=pltpu.VMEM)


def is_direct(n):
    return n in (1, 2, 4)


ORDERS = {
    "leaf_y": (3, 1, 2), "sep_sum": (2, 3, 1), "sep_y": (3, 1, 2), "top_sum": (2, 3, 1),
    "top_x": (2, 3, 1), "sep_t": (3, 1, 2), "sep_x": (3, 1, 2), "leaf_t": (3, 1, 2),
}
CROSSED = ("top_sum", "top_x")


class Exchange:
    def __init__(self, name, axis, n):
        self.axis, self.n, self.direct = axis, n, is_direct(n)
        self.steps = [0] + [d for d in ORDERS[name] if d < n]
        self.crossed = name in CROSSED

    def to(self, values, step):
        return (swap_cross if self.crossed else swap)(values, self.axis, self.n, step)


def swap(values, axis, n, step):
    return lax.ppermute(values, axis, [(i, i ^ step) for i in range(n)])


def swap_cross(values, axis, n, step):
    pairs = [(s * n + i, (1 - s) * n + (i ^ step)) for s in range(2) for i in range(n)]
    return lax.ppermute(values, ("sec", axis), pairs)


def gather(values, ex):
    if ex.direct:
        return [values] + [ex.to(values, d) for d in ex.steps[1:]]
    return [lax.all_gather(values, ex.axis, axis=0, tiled=True)]


def scatter_sum(blocks, ex):
    if ex.direct:
        return [blocks[0]] + [ex.to(block, d) for block, d in zip(blocks[1:], ex.steps[1:])]
    return [lax.psum_scatter(blocks[0], ex.axis, scatter_dimension=0, tiled=True)]


def own_half(n_col):
    sec = lax.axis_index("sec")
    return 1 - sec if is_direct(n_col) else sec


def nbytes(shape, dtype):
    size = jnp.dtype(dtype).itemsize
    for extent in shape:
        size *= extent
    return size


def call(kernel, outs, args, scratch=(), flops=0):
    total = sum(nbytes(s, t) for s, t in list(outs) + list(scratch)) + sum(nbytes(a.shape, a.dtype) for a in args)
    return pl.pallas_call(
        kernel,
        out_shape=tuple(jax.ShapeDtypeStruct(s, t) for s, t in outs),
        in_specs=[VMEM] * len(args),
        out_specs=(VMEM,) * len(outs),
        scratch_shapes=[pltpu.VMEM(s, t) for s, t in scratch],
        compiler_params=pltpu.CompilerParams(vmem_limit_bytes=total + (6 << 20)),
        cost_estimate=pl.CostEstimate(flops=flops, bytes_accessed=total, transcendentals=0),
    )(*args)


def place(ex):
    if not ex.direct:
        return lambda d: d
    me = lax.axis_index(ex.axis)
    return lambda d: me ^ d


def rows(index, size):
    return pl.ds(pl.multiple_of(index * size, size), size)


def dot(a, b):
    return jnp.dot(a, b, preferred_element_type=F32)


def dot_t(a, b):
    return lax.dot_general(a, b, (((0,), (0,)), ((), ())), preferred_element_type=F32)


def split(values):
    high = values.astype(BF)
    rest = values - high.astype(F32)
    mid = rest.astype(BF)
    return high, mid, (rest - mid.astype(F32)).astype(BF)


LEFT, RIGHT = (0, 1, 2, 0, 1, 0), (0, 0, 0, 1, 1, 2)


def apply_split(parts, right_side):
    right = split(right_side)
    return dot(parts, jnp.concatenate([right[k] for k in RIGHT], axis=0))


def store_split(out_ref, values):
    parts = split(values)
    width = values.shape[1]
    for place_of, k in enumerate(LEFT):
        out_ref[:, place_of * width : (place_of + 1) * width] = parts[k]


def total_of(refs):
    total = refs[0][...].astype(F32)
    for ref in refs[1:]:
        total = total + ref[...].astype(F32)
    return total


def lay_out(pieces, buf, ex):
    if not ex.direct:
        buf[...] = pieces[0][...]
        return
    at = place(ex)
    size = pieces[0].shape[0]
    for d, piece in zip(ex.steps, pieces):
        buf[rows(at(d), size), :] = piece[...]


def block_outs(ex, size, cols, own=True):
    if ex.direct:
        return [((size, cols), F32)] * own + [((size, cols), BF)] * (ex.n - 1)
    return [((ex.n * size, cols), F32)]


def emit_blocks(term, outs, ex):
    at = place(ex)
    if ex.direct:
        for d, out_ref in zip(reversed(ex.steps), reversed(outs)):
            out_ref[...] = term(at(d)).astype(out_ref.dtype)
    else:
        size = outs[0].shape[0] // ex.n
        for d in range(ex.n):
            outs[0][pl.ds(d * size, size), :] = term(d)


def leaf_first(leaf_inv, leaf_rhs):
    y = jnp.einsum("mab,mbn->man", leaf_inv, leaf_rhs.astype(F32), precision=lax.Precision.HIGHEST)
    y = y.reshape(-1, leaf_rhs.shape[2])
    return y, y.astype(BF)


def mask_tiles(tile_sets, masks, width):
    count = len(masks)
    n_col = masks[0].shape[0]

    def kernel(*refs):
        mask_refs, tile_refs, outs = refs[:count], refs[count : 2 * count], refs[2 * count :]
        for i in range(count):
            for k in range(masks[i].shape[2]):
                weight = jnp.broadcast_to(mask_refs[i][:, :, k : k + 1].astype(F32), (n_col, 1, width)).astype(BF)
                lanes = pl.ds(k * width, width)
                outs[i][:, :, lanes] = tile_refs[i][:, :, lanes] * weight

    return call(kernel, [(t.shape, BF) for t in tile_sets], [*masks, *tile_sets])


def split_transposes(inverse):
    blocks, width = inverse.shape[:2]

    def kernel(inv_ref, out_ref):
        for m in range(blocks):
            store_split(out_ref.at[m], inv_ref[m].T)

    return call(kernel, [((blocks, width, len(LEFT) * width), BF)], [inverse])[0]


def keep(values):
    def kernel(in_ref, out_ref):
        out_ref[...] = in_ref[...]

    return call(kernel, [(values.shape, values.dtype)], [values])[0]


def forward_blocks(tiles, pieces, source, target, width):
    cols = pieces[0].shape[1]
    depth = tiles.shape[1]
    count = len(pieces)

    def kernel(*refs):
        tile_ref, piece_refs, outs = refs[0], refs[1 : 1 + count], refs[1 + count : -1]
        buf = refs[-1]
        lay_out(piece_refs, buf, source)
        emit_blocks(lambda i: dot(tile_ref[rows(i, width), :], buf[...]), outs, target)

    outs = block_outs(target, width, cols, False) + [((depth, cols), BF)]
    got = call(kernel, outs, [tiles, *pieces], flops=2 * tiles.shape[0] * depth * cols)
    return blocks_of(got, target)


def blocks_of(got, ex):
    return ([None] if ex.direct else []) + list(got[:-1]), got[-1]


def own_forward(tiles, values, width):
    def kernel(tile_ref, value_ref, out_ref):
        out_ref[...] = dot(tile_ref[rows(lax.axis_index("col"), width), :], value_ref[...])

    return call(kernel, [((width, values.shape[1]), F32)], [tiles, values], flops=2 * width * values.size)[0]


def own_back(tiles, values, span, part=None):
    args = [tiles, values] + ([] if part is None else [part])

    def kernel(tile_ref, value_ref, *refs):
        own = rows(lax.axis_index("row"), span)
        out = dot_t(tile_ref[:, own], value_ref[...])
        refs[-1][...] = out if part is None else out + refs[0][own, :]

    return call(kernel, [((span, values.shape[1]), F32)], args, flops=2 * span * values.size)[0]


def plain_product(tiles, values, transposed):
    cols = values.shape[1]
    product = dot_t if transposed else dot

    def kernel(tile_ref, value_ref, out_ref):
        out_ref[...] = product(tile_ref[...], value_ref[...])

    shape = (tiles.shape[1] if transposed else tiles.shape[0], cols)
    return call(kernel, [(shape, F32)], [tiles, values], flops=2 * tiles.shape[0] * tiles.shape[1] * cols)[0]


def solve_forward(sums, right_side, inverse):
    total = sums[0].astype(F32)
    for piece in sums[1:]:
        total = total + piece.astype(F32)
    y = jnp.dot(inverse, right_side.astype(F32) - total, precision=lax.Precision.HIGHEST)
    return y, y.astype(BF)


def top_half(tiles, pieces, leaf_part, source, n_col, width, passed):
    cols = pieces[0].shape[1]
    half = cols // 2
    count = len(pieces)

    def kernel(*refs):
        tile_ref, piece_refs = refs[0], refs[1 : 1 + count]
        part_ref, out_ref, buf = refs[1 + count :]
        lay_out(piece_refs, buf, source)
        sec = lax.axis_index("sec")
        columns = rows(1 - sec if passed else sec, half)
        out_ref[...] = part_ref[:, columns] + dot(tile_ref[...], buf[:, columns])
        if is_direct(n_col):
            own = rows(lax.axis_index("col"), width)
            columns = rows(sec if passed else 1 - sec, half)
            out_ref[own, :] = part_ref[own, columns] + dot(tile_ref[own, :], buf[:, columns])

    return call(
        kernel,
        [((tiles.shape[0], half), F32)],
        [tiles, *pieces, leaf_part],
        scratch=[((tiles.shape[1], cols), BF)],
        flops=tiles.shape[0] * tiles.shape[1] * cols,
    )[0]


def add_sections(mine, other, target, width):
    half = mine.shape[1]

    def kernel(mine_ref, other_ref, *outs):
        emit_blocks(lambda i: mine_ref[rows(i, width), :] + other_ref[rows(i, width), :], outs, target)

    return call(kernel, block_outs(target, width, half), [mine, other])


def square_inverse(inverse):
    width = inverse.shape[0]

    def kernel(inv_ref, out_ref):
        value = inv_ref[...]
        store_split(
            out_ref,
            lax.dot_general(
                value, value, (((0,), (0,)), ((), ())),
                precision=lax.Precision.HIGHEST, preferred_element_type=F32,
            ),
        )

    return call(kernel, [((width, len(LEFT) * width), BF)], [inverse])[0]


def solve_top(sums, right_side, square, n_col):
    count = len(sums)
    half = right_side.shape[1] // 2

    def kernel(*refs):
        rhs_ref, sq_ref, x_ref, xb_ref = refs[count:]
        mine = rhs_ref[:, rows(own_half(n_col), half)].astype(F32)
        x = apply_split(sq_ref[...], mine - total_of(refs[:count]))
        x_ref[...] = x
        xb_ref[...] = x.astype(BF)

    shape = (right_side.shape[0], half)
    return call(kernel, [(shape, F32), (shape, BF)], [*sums, right_side, square])


def stack_pieces(pieces, source):
    if not source.direct:
        return pieces[0]

    def kernel(*refs):
        lay_out(refs[:-1], refs[-1], source)

    shape = (source.n * pieces[0].shape[0], pieces[0].shape[1])
    return call(kernel, [(shape, BF)], list(pieces))[0]


def join_halves(mine, other, n_col):
    half = mine.shape[1]

    def kernel(mine_ref, other_ref, out_ref):
        own = own_half(n_col)
        out_ref[:, rows(own, half)] = mine_ref[...]
        out_ref[:, rows(1 - own, half)] = other_ref[...]

    return call(kernel, [((mine.shape[0], 2 * half), mine.dtype)], [mine, other])[0]


def top_back_blocks(tiles, mine, other, target, n_col, width):
    half = mine.shape[1]

    def kernel(tile_ref, mine_ref, other_ref, *outs):
        buf = outs[-1]
        sec = lax.axis_index("sec")
        buf[:, rows(sec, half)] = mine_ref[...]
        buf[:, rows(1 - sec, half)] = other_ref[...]
        if is_direct(n_col):
            own = rows(lax.axis_index("col"), width)
            buf[own, rows(1 - sec, half)] = mine_ref[own, :]
            buf[own, rows(sec, half)] = other_ref[own, :]
        emit_blocks(lambda i: dot_t(tile_ref[:, rows(i, width)], buf[...]), outs[:-1], target)

    outs = block_outs(target, width, 2 * half, False) + [((mine.shape[0], 2 * half), BF)]
    got = call(kernel, outs, [tiles, mine, other], flops=4 * tiles.shape[0] * tiles.shape[1] * half)
    return blocks_of(got, target)


def back_blocks(tiles, pieces, top_part, source, target, span):
    cols = pieces[0].shape[1]
    count = len(pieces)

    def kernel(*refs):
        tile_ref, piece_refs, part_ref = refs[0], refs[1 : 1 + count], refs[1 + count]
        outs, buf = refs[2 + count : -1], refs[-1]
        lay_out(piece_refs, buf, source)
        emit_blocks(
            lambda i: part_ref[rows(i, span), :] + dot_t(tile_ref[:, rows(i, span)], buf[...]),
            outs, target,
        )

    outs = block_outs(target, span, cols, False) + [((tiles.shape[0], cols), BF)]
    got = call(kernel, outs, [tiles, *pieces, top_part], flops=2 * tiles.shape[0] * tiles.shape[1] * cols)
    return blocks_of(got, target)


def solve_back(sums, right_side, inverse):
    total = sums[0].astype(F32)
    for piece in sums[1:]:
        total = total + piece.astype(F32)
    x = jnp.einsum("ba,bn->an", inverse, right_side - total, precision=lax.Precision.HIGHEST)
    return x, x.astype(BF)


def solve_last(sums, right_side, inverse):
    count = len(sums)
    blocks, width = inverse.shape[:2]

    def kernel(*refs):
        y_ref, inv_ref, x_ref = refs[count:]
        rest = y_ref[...] - total_of(refs[:count])
        for m in range(blocks):
            x_ref[pl.ds(m * width, width), :] = apply_split(inv_ref[m], rest[m * width : (m + 1) * width])

    return call(kernel, [(right_side.shape, F32)], [*sums, right_side, inverse])[0]


def make_body(n_row, n_col):
    def body(leaf_rhs, sep_rhs, top_rhs, leaf_inv, sep_inv, top_inv,
             sep_leaf, top_leaf, top_sep, *masks):
        leaf_count, width, cols = leaf_rhs.shape[2], leaf_rhs.shape[4], leaf_rhs.shape[5]
        span = leaf_count * width

        ex = {name: Exchange(name, "row", n_row) for name in ("leaf_y", "sep_y", "sep_t", "leaf_t")}
        ex.update({name: Exchange(name, "col", n_col) for name in ("sep_sum", "top_sum", "top_x", "sep_x")})

        leaf_y, leaf_yb = leaf_first(leaf_inv[0, 0, :, 0], leaf_rhs[0, 0, :, 0])
        pieces = gather(leaf_yb, ex["leaf_y"])
        shaped = [mask.reshape(n_col, 1, -1) for mask in masks]
        sl = mask_tiles([sep_leaf.reshape(n_col, width, -1)], shaped[:1], width)[0].reshape(n_col * width, -1)
        blocks, leaf_col = forward_blocks(sl, pieces, ex["leaf_y"], ex["sep_sum"], width)
        top_leaf, top_sep, leaf_col = lax.optimization_barrier((top_leaf, top_sep, leaf_col))
        sums = scatter_sum(blocks, ex["sep_sum"])
        tops = [values.reshape(n_col, width, -1) for values in (top_leaf, top_sep)]
        tl, ts = [values.reshape(n_col * width, -1) for values in mask_tiles(tops, shaped[1:], width)]
        if is_direct(n_col):
            sums[0] = own_forward(sl, leaf_col, width)
        leaf_part = plain_product(tl, leaf_col, False)
        sums[0], ts, leaf_part = lax.optimization_barrier((sums[0], ts, leaf_part))
        sep_y, sep_yb = solve_forward(sums, sep_rhs[0, 0, 0], sep_inv[0, 0, 0])

        pieces = gather(sep_yb, ex["sep_y"])
        passed = swap(top_half(ts, pieces, leaf_part, ex["sep_y"], n_col, width, True), "sec", 2, 1)
        kept = top_half(ts, pieces, leaf_part, ex["sep_y"], n_col, width, False)
        sums = scatter_sum(add_sections(kept, passed, ex["top_sum"], width), ex["top_sum"])
        top_xh, top_xhb = solve_top(sums, top_rhs[0, 0], square_inverse(top_inv[0, 0]), n_col)
        top_stack = stack_pieces(gather(top_xhb, ex["top_x"]), ex["top_x"])

        blocks, top_row = top_back_blocks(ts, top_stack, swap(top_stack, "sec", 2, 1), ex["sep_t"], n_col, width)
        sums = scatter_sum(blocks, ex["sep_t"])
        if is_direct(n_row):
            sums[0] = own_back(ts, top_row, width)
        top_part = plain_product(tl, top_row, True)
        top_x = join_halves(top_xh, swap(top_xh, "sec", 2, 1), n_col)
        sep_x, sep_xb = solve_back(sums, sep_y, sep_inv[0, 0, 0])

        pieces = gather(sep_xb, ex["sep_x"])
        blocks, sep_row = back_blocks(sl, pieces, top_part, ex["sep_x"], ex["leaf_t"], span)
        sums = scatter_sum(blocks, ex["leaf_t"])
        if is_direct(n_row):
            sums[0] = own_back(sl, sep_row, span, top_part)
        leaf_x = solve_last(sums, leaf_y, split_transposes(leaf_inv[0, 0, :, 0]))
        return (
            leaf_x.reshape(1, 1, leaf_count, 1, width, cols),
            keep(sep_x)[None, None, None],
            top_x[None, None],
        )

    return body


def solution(mesh):
    in_specs = (
        P("sec", "row", None, "col", None, None),
        P("sec", "row", "col", None, None),
        P("row", "col", None, None),
        P("sec", "row", None, "col", None, None),
        P("sec", "row", "col", None, None),
        P("row", "col", None, None),
        P("sec", "row", None, None, None, None, "col", None),
        P("sec", "row", None, None, None, None, "col", None),
        P("sec", "row", None, None, None, "col", None),
        P("sec", "row", None, None, None, "col"),
        P("sec", "row", None, None, None, "col"),
        P("sec", "row", None, None, "col"),
    )
    out_specs = (
        P("sec", "row", None, "col", None, None),
        P("sec", "row", "col", None, None),
        P("row", "col", None, None),
    )
    body = make_body(mesh.shape["row"], mesh.shape["col"])
    return jax.shard_map(body, mesh=mesh, in_specs=in_specs, out_specs=out_specs, check_vma=False)
```

```python
import jax
import jax.numpy as jnp
from jax import lax
from jax.experimental import pallas as pl
from jax.experimental.pallas import tpu as pltpu
from jax.sharding import PartitionSpec as P

BF = jnp.bfloat16
F32 = jnp.float32
VMEM = pl.BlockSpec(memory_space=pltpu.VMEM)


def is_direct(n):
    return n in (1, 2, 4)


ORDERS = {
    "leaf_y": (3, 1, 2), "sep_sum": (2, 3, 1), "sep_y": (3, 1, 2), "top_sum": (2, 3, 1),
    "top_x": (2, 3, 1), "sep_t": (3, 1, 2), "sep_x": (3, 1, 2), "leaf_t": (3, 1, 2),
}
CROSSED = ("top_sum", "top_x")


class Exchange:
    def __init__(self, name, axis, n):
        self.axis, self.n, self.direct = axis, n, is_direct(n)
        self.steps = [0] + [d for d in ORDERS[name] if d < n]
        self.crossed = name in CROSSED

    def to(self, values, step):
        return (swap_cross if self.crossed else swap)(values, self.axis, self.n, step)


def swap(values, axis, n, step):
    return lax.ppermute(values, axis, [(i, i ^ step) for i in range(n)])


def swap_cross(values, axis, n, step):
    pairs = [(s * n + i, (1 - s) * n + (i ^ step)) for s in range(2) for i in range(n)]
    return lax.ppermute(values, ("sec", axis), pairs)


def gather(values, ex):
    if ex.direct:
        return [values] + [ex.to(values, d) for d in ex.steps[1:]]
    return [lax.all_gather(values, ex.axis, axis=0, tiled=True)]


def scatter_sum(blocks, ex):
    if ex.direct:
        return [blocks[0]] + [ex.to(block, d) for block, d in zip(blocks[1:], ex.steps[1:])]
    return [lax.psum_scatter(blocks[0], ex.axis, scatter_dimension=0, tiled=True)]


def own_half(n_col):
    sec = lax.axis_index("sec")
    return 1 - sec if is_direct(n_col) else sec


def nbytes(shape, dtype):
    size = jnp.dtype(dtype).itemsize
    for extent in shape:
        size *= extent
    return size


def call(kernel, outs, args, scratch=(), flops=0):
    total = sum(nbytes(s, t) for s, t in list(outs) + list(scratch)) + sum(nbytes(a.shape, a.dtype) for a in args)
    return pl.pallas_call(
        kernel,
        out_shape=tuple(jax.ShapeDtypeStruct(s, t) for s, t in outs),
        in_specs=[VMEM] * len(args),
        out_specs=(VMEM,) * len(outs),
        scratch_shapes=[pltpu.VMEM(s, t) for s, t in scratch],
        compiler_params=pltpu.CompilerParams(vmem_limit_bytes=total + (6 << 20)),
        cost_estimate=pl.CostEstimate(flops=flops, bytes_accessed=total, transcendentals=0),
    )(*args)


def place(ex):
    if not ex.direct:
        return lambda d: d
    me = lax.axis_index(ex.axis)
    return lambda d: me ^ d


def rows(index, size):
    return pl.ds(pl.multiple_of(index * size, size), size)


def dot(a, b):
    return jnp.dot(a, b, preferred_element_type=F32)


def dot_t(a, b):
    return lax.dot_general(a, b, (((0,), (0,)), ((), ())), preferred_element_type=F32)


def split(values):
    high = values.astype(BF)
    rest = values - high.astype(F32)
    mid = rest.astype(BF)
    return high, mid, (rest - mid.astype(F32)).astype(BF)


LEFT, RIGHT = (0, 1, 2, 0, 1, 0), (0, 0, 0, 1, 1, 2)


def apply_split(parts, right_side):
    right = split(right_side)
    return dot(parts, jnp.concatenate([right[k] for k in RIGHT], axis=0))


def store_split(out_ref, values):
    parts = split(values)
    width = values.shape[1]
    for place_of, k in enumerate(LEFT):
        out_ref[:, place_of * width : (place_of + 1) * width] = parts[k]


def total_of(refs):
    total = refs[0][...].astype(F32)
    for ref in refs[1:]:
        total = total + ref[...].astype(F32)
    return total


def lay_out(pieces, buf, ex):
    if not ex.direct:
        buf[...] = pieces[0][...]
        return
    at = place(ex)
    size = pieces[0].shape[0]
    for d, piece in zip(ex.steps, pieces):
        buf[rows(at(d), size), :] = piece[...]


def block_outs(ex, size, cols, own=True):
    if ex.direct:
        return [((size, cols), F32)] * own + [((size, cols), BF)] * (ex.n - 1)
    return [((ex.n * size, cols), F32)]


def emit_blocks(term, outs, ex):
    at = place(ex)
    if ex.direct:
        for d, out_ref in zip(reversed(ex.steps), reversed(outs)):
            out_ref[...] = term(at(d)).astype(out_ref.dtype)
    else:
        size = outs[0].shape[0] // ex.n
        for d in range(ex.n):
            outs[0][pl.ds(d * size, size), :] = term(d)


def leaf_first(leaf_inv, leaf_rhs):
    y = jnp.einsum("mab,mbn->man", leaf_inv, leaf_rhs.astype(F32), precision=lax.Precision.HIGHEST)
    y = y.reshape(-1, leaf_rhs.shape[2])
    return y, y.astype(BF)


def mask_tiles(tile_sets, masks, width, carried=()):
    count = len(masks)
    n_col = masks[0].shape[0]

    def kernel(*refs):
        mask_refs, tile_refs = refs[:count], refs[count : 2 * count]
        later, outs = refs[2 * count : 2 * count + len(carried)], refs[2 * count + len(carried) :]
        for in_ref, out_ref in zip(later, outs[count:]):
            out_ref[...] = in_ref[...]
        for i in range(count):
            for k in range(masks[i].shape[2]):
                weight = jnp.broadcast_to(mask_refs[i][:, :, k : k + 1].astype(F32), (n_col, 1, width)).astype(BF)
                lanes = pl.ds(k * width, width)
                outs[i][:, :, lanes] = tile_refs[i][:, :, lanes] * weight

    outs = [(t.shape, BF) for t in tile_sets] + [(m.shape, m.dtype) for m in carried]
    return call(kernel, outs, [*masks, *tile_sets, *carried])


def split_transposes(inverse):
    blocks, width = inverse.shape[:2]

    def kernel(inv_ref, out_ref):
        for m in range(blocks):
            store_split(out_ref.at[m], inv_ref[m].T)

    return call(kernel, [((blocks, width, len(LEFT) * width), BF)], [inverse])[0]


def keep(values):
    def kernel(in_ref, out_ref):
        out_ref[...] = in_ref[...]

    return call(kernel, [(values.shape, values.dtype)], [values])[0]


def forward_blocks(tiles, pieces, source, target, width):
    cols = pieces[0].shape[1]
    depth = tiles.shape[1]
    count = len(pieces)

    def kernel(*refs):
        tile_ref, piece_refs, outs = refs[0], refs[1 : 1 + count], refs[1 + count : -1]
        buf = refs[-1]
        lay_out(piece_refs, buf, source)
        emit_blocks(lambda i: dot(tile_ref[rows(i, width), :], buf[...]), outs, target)

    outs = block_outs(target, width, cols, False) + [((depth, cols), BF)]
    got = call(kernel, outs, [tiles, *pieces], flops=2 * tiles.shape[0] * depth * cols)
    return blocks_of(got, target)


def blocks_of(got, ex):
    return ([None] if ex.direct else []) + list(got[:-1]), got[-1]


def own_forward(tiles, values, width):
    def kernel(tile_ref, value_ref, out_ref):
        out_ref[...] = dot(tile_ref[rows(lax.axis_index("col"), width), :], value_ref[...])

    return call(kernel, [((width, values.shape[1]), F32)], [tiles, values], flops=2 * width * values.size)[0]


def own_back(tiles, values, span, part=None):
    args = [tiles, values] + ([] if part is None else [part])

    def kernel(tile_ref, value_ref, *refs):
        own = rows(lax.axis_index("row"), span)
        out = dot_t(tile_ref[:, own], value_ref[...])
        refs[-1][...] = out if part is None else out + refs[0][own, :]

    return call(kernel, [((span, values.shape[1]), F32)], args, flops=2 * span * values.size)[0]


def plain_product(tiles, values, transposed):
    cols = values.shape[1]
    product = dot_t if transposed else dot

    def kernel(tile_ref, value_ref, out_ref):
        out_ref[...] = product(tile_ref[...], value_ref[...])

    shape = (tiles.shape[1] if transposed else tiles.shape[0], cols)
    return call(kernel, [(shape, F32)], [tiles, values], flops=2 * tiles.shape[0] * tiles.shape[1] * cols)[0]


def solve_forward(sums, right_side, inverse):
    total = sums[0].astype(F32)
    for piece in sums[1:]:
        total = total + piece.astype(F32)
    y = jnp.dot(inverse, right_side.astype(F32) - total, precision=lax.Precision.HIGHEST)
    return y, y.astype(BF)


def top_half(tiles, pieces, leaf_part, source, n_col, width, passed):
    cols = pieces[0].shape[1]
    half = cols // 2
    count = len(pieces)

    def kernel(*refs):
        tile_ref, piece_refs = refs[0], refs[1 : 1 + count]
        part_ref, out_ref, buf = refs[1 + count :]
        lay_out(piece_refs, buf, source)
        sec = lax.axis_index("sec")
        columns = rows(1 - sec if passed else sec, half)
        out_ref[...] = part_ref[:, columns] + dot(tile_ref[...], buf[:, columns])
        if is_direct(n_col):
            own = rows(lax.axis_index("col"), width)
            columns = rows(sec if passed else 1 - sec, half)
            out_ref[own, :] = part_ref[own, columns] + dot(tile_ref[own, :], buf[:, columns])

    return call(
        kernel,
        [((tiles.shape[0], half), F32)],
        [tiles, *pieces, leaf_part],
        scratch=[((tiles.shape[1], cols), BF)],
        flops=tiles.shape[0] * tiles.shape[1] * cols,
    )[0]


def add_sections(mine, other, target, width):
    half = mine.shape[1]

    def kernel(mine_ref, other_ref, *outs):
        emit_blocks(lambda i: mine_ref[rows(i, width), :] + other_ref[rows(i, width), :], outs, target)

    return call(kernel, block_outs(target, width, half), [mine, other])


def square_inverse(inverse):
    width = inverse.shape[0]

    def kernel(inv_ref, out_ref):
        value = inv_ref[...]
        store_split(
            out_ref,
            lax.dot_general(
                value, value, (((0,), (0,)), ((), ())),
                precision=lax.Precision.HIGHEST, preferred_element_type=F32,
            ),
        )

    return call(kernel, [((width, len(LEFT) * width), BF)], [inverse])[0]


def solve_top(sums, right_side, square, n_col):
    count = len(sums)
    half = right_side.shape[1] // 2

    def kernel(*refs):
        rhs_ref, sq_ref, x_ref, xb_ref = refs[count:]
        mine = rhs_ref[:, rows(own_half(n_col), half)].astype(F32)
        x = apply_split(sq_ref[...], mine - total_of(refs[:count]))
        x_ref[...] = x
        xb_ref[...] = x.astype(BF)

    shape = (right_side.shape[0], half)
    return call(kernel, [(shape, F32), (shape, BF)], [*sums, right_side, square])


def stack_pieces(pieces, source):
    if not source.direct:
        return pieces[0]

    def kernel(*refs):
        lay_out(refs[:-1], refs[-1], source)

    shape = (source.n * pieces[0].shape[0], pieces[0].shape[1])
    return call(kernel, [(shape, BF)], list(pieces))[0]


def join_halves(mine, other, n_col):
    half = mine.shape[1]

    def kernel(mine_ref, other_ref, out_ref):
        own = own_half(n_col)
        out_ref[:, rows(own, half)] = mine_ref[...]
        out_ref[:, rows(1 - own, half)] = other_ref[...]

    return call(kernel, [((mine.shape[0], 2 * half), mine.dtype)], [mine, other])[0]


def top_back_blocks(tiles, mine, other, target, n_col, width):
    half = mine.shape[1]

    def kernel(tile_ref, mine_ref, other_ref, *outs):
        buf = outs[-1]
        sec = lax.axis_index("sec")
        buf[:, rows(sec, half)] = mine_ref[...]
        buf[:, rows(1 - sec, half)] = other_ref[...]
        if is_direct(n_col):
            own = rows(lax.axis_index("col"), width)
            buf[own, rows(1 - sec, half)] = mine_ref[own, :]
            buf[own, rows(sec, half)] = other_ref[own, :]
        emit_blocks(lambda i: dot_t(tile_ref[:, rows(i, width)], buf[...]), outs[:-1], target)

    outs = block_outs(target, width, 2 * half, False) + [((mine.shape[0], 2 * half), BF)]
    got = call(kernel, outs, [tiles, mine, other], flops=4 * tiles.shape[0] * tiles.shape[1] * half)
    return blocks_of(got, target)


def back_blocks(tiles, pieces, top_part, source, target, span):
    cols = pieces[0].shape[1]
    count = len(pieces)

    def kernel(*refs):
        tile_ref, piece_refs, part_ref = refs[0], refs[1 : 1 + count], refs[1 + count]
        outs, buf = refs[2 + count : -1], refs[-1]
        lay_out(piece_refs, buf, source)
        emit_blocks(
            lambda i: part_ref[rows(i, span), :] + dot_t(tile_ref[:, rows(i, span)], buf[...]),
            outs, target,
        )

    outs = block_outs(target, span, cols, False) + [((tiles.shape[0], cols), BF)]
    got = call(kernel, outs, [tiles, *pieces, top_part], flops=2 * tiles.shape[0] * tiles.shape[1] * cols)
    return blocks_of(got, target)


def solve_back(sums, right_side, inverse):
    total = sums[0].astype(F32)
    for piece in sums[1:]:
        total = total + piece.astype(F32)
    x = jnp.einsum("ba,bn->an", inverse, right_side - total, precision=lax.Precision.HIGHEST)
    return x, x.astype(BF)


def solve_last(sums, right_side, inverse):
    count = len(sums)
    blocks, width = inverse.shape[:2]

    def kernel(*refs):
        y_ref, inv_ref, x_ref = refs[count:]
        rest = y_ref[...] - total_of(refs[:count])
        for m in range(blocks):
            x_ref[pl.ds(m * width, width), :] = apply_split(inv_ref[m], rest[m * width : (m + 1) * width])

    return call(kernel, [(right_side.shape, F32)], [*sums, right_side, inverse])[0]


def make_body(n_row, n_col):
    def body(leaf_rhs, sep_rhs, top_rhs, leaf_inv, sep_inv, top_inv,
             sep_leaf, top_leaf, top_sep, *masks):
        leaf_count, width, cols = leaf_rhs.shape[2], leaf_rhs.shape[4], leaf_rhs.shape[5]
        span = leaf_count * width

        ex = {name: Exchange(name, "row", n_row) for name in ("leaf_y", "sep_y", "sep_t", "leaf_t")}
        ex.update({name: Exchange(name, "col", n_col) for name in ("sep_sum", "top_sum", "top_x", "sep_x")})

        leaf_y, leaf_yb = leaf_first(leaf_inv[0, 0, :, 0], leaf_rhs[0, 0, :, 0])
        pieces = gather(leaf_yb, ex["leaf_y"])
        shaped = [mask.reshape(n_col, 1, -1) for mask in masks]
        sl, *shaped[1:] = mask_tiles([sep_leaf.reshape(n_col, width, -1)], shaped[:1], width, shaped[1:])
        sl = sl.reshape(n_col * width, -1)
        blocks, leaf_col = forward_blocks(sl, pieces, ex["leaf_y"], ex["sep_sum"], width)
        top_leaf, top_sep, leaf_col = lax.optimization_barrier((top_leaf, top_sep, leaf_col))
        sums = scatter_sum(blocks, ex["sep_sum"])
        tops = [values.reshape(n_col, width, -1) for values in (top_leaf, top_sep)]
        tl, ts = [values.reshape(n_col * width, -1) for values in mask_tiles(tops, shaped[1:], width)]
        if is_direct(n_col):
            sums[0] = own_forward(sl, leaf_col, width)
        leaf_part = plain_product(tl, leaf_col, False)
        sums[0], ts, leaf_part = lax.optimization_barrier((sums[0], ts, leaf_part))
        sep_y, sep_yb = solve_forward(sums, sep_rhs[0, 0, 0], sep_inv[0, 0, 0])

        pieces = gather(sep_yb, ex["sep_y"])
        passed = swap(top_half(ts, pieces, leaf_part, ex["sep_y"], n_col, width, True), "sec", 2, 1)
        kept = top_half(ts, pieces, leaf_part, ex["sep_y"], n_col, width, False)
        sums = scatter_sum(add_sections(kept, passed, ex["top_sum"], width), ex["top_sum"])
        top_xh, top_xhb = solve_top(sums, top_rhs[0, 0], square_inverse(top_inv[0, 0]), n_col)
        top_stack = stack_pieces(gather(top_xhb, ex["top_x"]), ex["top_x"])

        blocks, top_row = top_back_blocks(ts, top_stack, swap(top_stack, "sec", 2, 1), ex["sep_t"], n_col, width)
        sums = scatter_sum(blocks, ex["sep_t"])
        if is_direct(n_row):
            sums[0] = own_back(ts, top_row, width)
        top_part = plain_product(tl, top_row, True)
        top_x = join_halves(top_xh, swap(top_xh, "sec", 2, 1), n_col)
        sep_x, sep_xb = solve_back(sums, sep_y, sep_inv[0, 0, 0])

        pieces = gather(sep_xb, ex["sep_x"])
        blocks, sep_row = back_blocks(sl, pieces, top_part, ex["sep_x"], ex["leaf_t"], span)
        sums = scatter_sum(blocks, ex["leaf_t"])
        if is_direct(n_row):
            sums[0] = own_back(sl, sep_row, span, top_part)
        leaf_x = solve_last(sums, leaf_y, split_transposes(leaf_inv[0, 0, :, 0]))
        return (
            leaf_x.reshape(1, 1, leaf_count, 1, width, cols),
            keep(sep_x)[None, None, None],
            top_x[None, None],
        )

    return body


def solution(mesh):
    in_specs = (
        P("sec", "row", None, "col", None, None),
        P("sec", "row", "col", None, None),
        P("row", "col", None, None),
        P("sec", "row", None, "col", None, None),
        P("sec", "row", "col", None, None),
        P("row", "col", None, None),
        P("sec", "row", None, None, None, None, "col", None),
        P("sec", "row", None, None, None, None, "col", None),
        P("sec", "row", None, None, None, "col", None),
        P("sec", "row", None, None, None, "col"),
        P("sec", "row", None, None, None, "col"),
        P("sec", "row", None, None, "col"),
    )
    out_specs = (
        P("sec", "row", None, "col", None, None),
        P("sec", "row", "col", None, None),
        P("row", "col", None, None),
    )
    body = make_body(mesh.shape["row"], mesh.shape["col"])
    return jax.shard_map(body, mesh=mesh, in_specs=in_specs, out_specs=out_specs, check_vma=False)
```

```python
import jax
import jax.numpy as jnp
from jax import lax
from jax.experimental import pallas as pl
from jax.experimental.pallas import tpu as pltpu
from jax.sharding import PartitionSpec as P

BF = jnp.bfloat16
F32 = jnp.float32
VMEM = pl.BlockSpec(memory_space=pltpu.VMEM)


def is_direct(n):
    return n in (1, 2, 4)


ORDERS = {
    "leaf_y": (3, 1, 2), "sep_sum": (2, 3, 1), "sep_y": (3, 1, 2), "top_sum": (2, 3, 1),
    "top_x": (2, 3, 1), "sep_t": (3, 1, 2), "sep_x": (3, 1, 2), "leaf_t": (3, 1, 2),
}
CROSSED = ("top_sum", "top_x")


class Exchange:
    def __init__(self, name, axis, n):
        self.axis, self.n, self.direct = axis, n, is_direct(n)
        self.steps = [0] + [d for d in ORDERS[name] if d < n]
        self.crossed = name in CROSSED

    def to(self, values, step):
        return (swap_cross if self.crossed else swap)(values, self.axis, self.n, step)


def swap(values, axis, n, step):
    return lax.ppermute(values, axis, [(i, i ^ step) for i in range(n)])


def swap_cross(values, axis, n, step):
    pairs = [(s * n + i, (1 - s) * n + (i ^ step)) for s in range(2) for i in range(n)]
    return lax.ppermute(values, ("sec", axis), pairs)


def gather(values, ex):
    if ex.direct:
        return [values] + [ex.to(values, d) for d in ex.steps[1:]]
    return [lax.all_gather(values, ex.axis, axis=0, tiled=True)]


def scatter_sum(blocks, ex):
    if ex.direct:
        return [blocks[0]] + [ex.to(block, d) for block, d in zip(blocks[1:], ex.steps[1:])]
    return [lax.psum_scatter(blocks[0], ex.axis, scatter_dimension=0, tiled=True)]


def own_half(n_col):
    sec = lax.axis_index("sec")
    return 1 - sec if is_direct(n_col) else sec


def nbytes(shape, dtype):
    size = jnp.dtype(dtype).itemsize
    for extent in shape:
        size *= extent
    return size


def call(kernel, outs, args, scratch=(), flops=0):
    total = sum(nbytes(s, t) for s, t in list(outs) + list(scratch)) + sum(nbytes(a.shape, a.dtype) for a in args)
    return pl.pallas_call(
        kernel,
        out_shape=tuple(jax.ShapeDtypeStruct(s, t) for s, t in outs),
        in_specs=[VMEM] * len(args),
        out_specs=(VMEM,) * len(outs),
        scratch_shapes=[pltpu.VMEM(s, t) for s, t in scratch],
        compiler_params=pltpu.CompilerParams(vmem_limit_bytes=total + (2 << 20)),
        cost_estimate=pl.CostEstimate(flops=flops, bytes_accessed=total, transcendentals=0),
    )(*args)


def place(ex):
    if not ex.direct:
        return lambda d: d
    me = lax.axis_index(ex.axis)
    return lambda d: me ^ d


def rows(index, size):
    return pl.ds(pl.multiple_of(index * size, size), size)


def dot(a, b):
    return jnp.dot(a, b, preferred_element_type=F32)


def dot_t(a, b):
    return lax.dot_general(a, b, (((0,), (0,)), ((), ())), preferred_element_type=F32)


def split(values):
    high = values.astype(BF)
    rest = values - high.astype(F32)
    mid = rest.astype(BF)
    return high, mid, (rest - mid.astype(F32)).astype(BF)


LEFT, RIGHT = (0, 1, 2, 0, 1, 0), (0, 0, 0, 1, 1, 2)


def apply_split(parts, right_side):
    right = split(right_side)
    return dot(parts, jnp.concatenate([right[k] for k in RIGHT], axis=0))


def store_split(out_ref, values):
    parts = split(values)
    width = values.shape[1]
    for place_of, k in enumerate(LEFT):
        out_ref[:, place_of * width : (place_of + 1) * width] = parts[k]


def total_of(refs):
    total = refs[0][...].astype(F32)
    for ref in refs[1:]:
        total = total + ref[...].astype(F32)
    return total


def lay_out(pieces, buf, ex):
    if not ex.direct:
        buf[...] = pieces[0][...]
        return
    at = place(ex)
    size = pieces[0].shape[0]
    for d, piece in zip(ex.steps, pieces):
        buf[rows(at(d), size), :] = piece[...]


def block_outs(ex, size, cols, own=True):
    if ex.direct:
        return [((size, cols), F32)] * own + [((size, cols), BF)] * (ex.n - 1)
    return [((ex.n * size, cols), F32)]


def emit_blocks(term, outs, ex):
    at = place(ex)
    if ex.direct:
        for d, out_ref in zip(reversed(ex.steps), reversed(outs)):
            out_ref[...] = term(at(d)).astype(out_ref.dtype)
    else:
        size = outs[0].shape[0] // ex.n
        for d in range(ex.n):
            outs[0][pl.ds(d * size, size), :] = term(d)


def leaf_first(leaf_inv, leaf_rhs):
    y = jnp.einsum("mab,mbn->man", leaf_inv, leaf_rhs.astype(F32), precision=lax.Precision.HIGHEST)
    y = y.reshape(-1, leaf_rhs.shape[2])
    return y, y.astype(BF)


def mask_tiles(tile_sets, masks, width):
    count = len(masks)
    n_col = masks[0].shape[0]

    def kernel(*refs):
        mask_refs, tile_refs, outs = refs[:count], refs[count : 2 * count], refs[2 * count :]
        for i in range(count):
            for k in range(masks[i].shape[2]):
                weight = jnp.broadcast_to(mask_refs[i][:, :, k : k + 1].astype(F32), (n_col, 1, width)).astype(BF)
                lanes = pl.ds(k * width, width)
                outs[i][:, :, lanes] = tile_refs[i][:, :, lanes] * weight

    return call(kernel, [(t.shape, BF) for t in tile_sets], [*masks, *tile_sets])


def split_transposes(inverse):
    blocks, width = inverse.shape[:2]

    def kernel(inv_ref, out_ref):
        for m in range(blocks):
            store_split(out_ref.at[m], inv_ref[m].T)

    return call(kernel, [((blocks, width, len(LEFT) * width), BF)], [inverse])[0]


def keep(values):
    def kernel(in_ref, out_ref):
        out_ref[...] = in_ref[...]

    return call(kernel, [(values.shape, values.dtype)], [values])[0]


def forward_blocks(tiles, pieces, source, target, width):
    cols = pieces[0].shape[1]
    depth = tiles.shape[1]
    count = len(pieces)

    def kernel(*refs):
        tile_ref, piece_refs, outs = refs[0], refs[1 : 1 + count], refs[1 + count : -1]
        buf = refs[-1]
        lay_out(piece_refs, buf, source)
        emit_blocks(lambda i: dot(tile_ref[rows(i, width), :], buf[...]), outs, target)

    outs = block_outs(target, width, cols, False) + [((depth, cols), BF)]
    got = call(kernel, outs, [tiles, *pieces], flops=2 * tiles.shape[0] * depth * cols)
    return blocks_of(got, target)


def blocks_of(got, ex):
    return ([None] if ex.direct else []) + list(got[:-1]), got[-1]


def own_forward(tiles, values, width):
    def kernel(tile_ref, value_ref, out_ref):
        out_ref[...] = dot(tile_ref[rows(lax.axis_index("col"), width), :], value_ref[...])

    return call(kernel, [((width, values.shape[1]), F32)], [tiles, values], flops=2 * width * values.size)[0]


def own_back(tiles, values, span, part=None):
    args = [tiles, values] + ([] if part is None else [part])

    def kernel(tile_ref, value_ref, *refs):
        own = rows(lax.axis_index("row"), span)
        out = dot_t(tile_ref[:, own], value_ref[...])
        refs[-1][...] = out if part is None else out + refs[0][own, :]

    return call(kernel, [((span, values.shape[1]), F32)], args, flops=2 * span * values.size)[0]


def plain_product(tiles, values, transposed):
    cols = values.shape[1]
    product = dot_t if transposed else dot

    def kernel(tile_ref, value_ref, out_ref):
        out_ref[...] = product(tile_ref[...], value_ref[...])

    shape = (tiles.shape[1] if transposed else tiles.shape[0], cols)
    return call(kernel, [(shape, F32)], [tiles, values], flops=2 * tiles.shape[0] * tiles.shape[1] * cols)[0]


def solve_forward(sums, right_side, inverse):
    total = sums[0].astype(F32)
    for piece in sums[1:]:
        total = total + piece.astype(F32)
    y = jnp.dot(inverse, right_side.astype(F32) - total, precision=lax.Precision.HIGHEST)
    return y, y.astype(BF)


def top_half(tiles, pieces, leaf_part, source, n_col, width, passed):
    cols = pieces[0].shape[1]
    half = cols // 2
    count = len(pieces)

    def kernel(*refs):
        tile_ref, piece_refs = refs[0], refs[1 : 1 + count]
        part_ref, out_ref, buf = refs[1 + count :]
        lay_out(piece_refs, buf, source)
        sec = lax.axis_index("sec")
        columns = rows(1 - sec if passed else sec, half)
        out_ref[...] = part_ref[:, columns] + dot(tile_ref[...], buf[:, columns])
        if is_direct(n_col):
            own = rows(lax.axis_index("col"), width)
            columns = rows(sec if passed else 1 - sec, half)
            out_ref[own, :] = part_ref[own, columns] + dot(tile_ref[own, :], buf[:, columns])

    return call(
        kernel,
        [((tiles.shape[0], half), F32)],
        [tiles, *pieces, leaf_part],
        scratch=[((tiles.shape[1], cols), BF)],
        flops=tiles.shape[0] * tiles.shape[1] * cols,
    )[0]


def add_sections(mine, other, target, width):
    half = mine.shape[1]

    def kernel(mine_ref, other_ref, *outs):
        emit_blocks(lambda i: mine_ref[rows(i, width), :] + other_ref[rows(i, width), :], outs, target)

    return call(kernel, block_outs(target, width, half), [mine, other])


def square_inverse(inverse):
    width = inverse.shape[0]

    def kernel(inv_ref, out_ref):
        value = inv_ref[...]
        store_split(
            out_ref,
            lax.dot_general(
                value, value, (((0,), (0,)), ((), ())),
                precision=lax.Precision.HIGHEST, preferred_element_type=F32,
            ),
        )

    return call(kernel, [((width, len(LEFT) * width), BF)], [inverse])[0]


def solve_top(sums, right_side, square, n_col):
    count = len(sums)
    half = right_side.shape[1] // 2

    def kernel(*refs):
        rhs_ref, sq_ref, x_ref, xb_ref = refs[count:]
        mine = rhs_ref[:, rows(own_half(n_col), half)].astype(F32)
        x = apply_split(sq_ref[...], mine - total_of(refs[:count]))
        x_ref[...] = x
        xb_ref[...] = x.astype(BF)

    shape = (right_side.shape[0], half)
    return call(kernel, [(shape, F32), (shape, BF)], [*sums, right_side, square])


def stack_pieces(pieces, source):
    if not source.direct:
        return pieces[0]

    def kernel(*refs):
        lay_out(refs[:-1], refs[-1], source)

    shape = (source.n * pieces[0].shape[0], pieces[0].shape[1])
    return call(kernel, [(shape, BF)], list(pieces))[0]


def join_halves(mine, other, n_col):
    half = mine.shape[1]

    def kernel(mine_ref, other_ref, out_ref):
        own = own_half(n_col)
        out_ref[:, rows(own, half)] = mine_ref[...]
        out_ref[:, rows(1 - own, half)] = other_ref[...]

    return call(kernel, [((mine.shape[0], 2 * half), mine.dtype)], [mine, other])[0]


def top_back_blocks(tiles, mine, other, target, n_col, width):
    half = mine.shape[1]

    def kernel(tile_ref, mine_ref, other_ref, *outs):
        buf = outs[-1]
        sec = lax.axis_index("sec")
        buf[:, rows(sec, half)] = mine_ref[...]
        buf[:, rows(1 - sec, half)] = other_ref[...]
        if is_direct(n_col):
            own = rows(lax.axis_index("col"), width)
            buf[own, rows(1 - sec, half)] = mine_ref[own, :]
            buf[own, rows(sec, half)] = other_ref[own, :]
        emit_blocks(lambda i: dot_t(tile_ref[:, rows(i, width)], buf[...]), outs[:-1], target)

    outs = block_outs(target, width, 2 * half, False) + [((mine.shape[0], 2 * half), BF)]
    got = call(kernel, outs, [tiles, mine, other], flops=4 * tiles.shape[0] * tiles.shape[1] * half)
    return blocks_of(got, target)


def back_blocks(tiles, pieces, top_part, source, target, span):
    cols = pieces[0].shape[1]
    count = len(pieces)

    def kernel(*refs):
        tile_ref, piece_refs, part_ref = refs[0], refs[1 : 1 + count], refs[1 + count]
        outs, buf = refs[2 + count : -1], refs[-1]
        lay_out(piece_refs, buf, source)
        emit_blocks(
            lambda i: part_ref[rows(i, span), :] + dot_t(tile_ref[:, rows(i, span)], buf[...]),
            outs, target,
        )

    outs = block_outs(target, span, cols, False) + [((tiles.shape[0], cols), BF)]
    got = call(kernel, outs, [tiles, *pieces, top_part], flops=2 * tiles.shape[0] * tiles.shape[1] * cols)
    return blocks_of(got, target)


def solve_back(sums, right_side, inverse):
    total = sums[0].astype(F32)
    for piece in sums[1:]:
        total = total + piece.astype(F32)
    x = jnp.einsum("ba,bn->an", inverse, right_side - total, precision=lax.Precision.HIGHEST)
    return x, x.astype(BF)


def solve_last(sums, right_side, inverse):
    count = len(sums)
    blocks, width = inverse.shape[:2]

    def kernel(*refs):
        y_ref, inv_ref, x_ref = refs[count:]
        rest = y_ref[...] - total_of(refs[:count])
        for m in range(blocks):
            x_ref[pl.ds(m * width, width), :] = apply_split(inv_ref[m], rest[m * width : (m + 1) * width])

    return call(kernel, [(right_side.shape, F32)], [*sums, right_side, inverse])[0]


def make_body(n_row, n_col):
    def body(leaf_rhs, sep_rhs, top_rhs, leaf_inv, sep_inv, top_inv,
             sep_leaf, top_leaf, top_sep, *masks):
        leaf_count, width, cols = leaf_rhs.shape[2], leaf_rhs.shape[4], leaf_rhs.shape[5]
        span = leaf_count * width

        ex = {name: Exchange(name, "row", n_row) for name in ("leaf_y", "sep_y", "sep_t", "leaf_t")}
        ex.update({name: Exchange(name, "col", n_col) for name in ("sep_sum", "top_sum", "top_x", "sep_x")})

        leaf_y, leaf_yb = leaf_first(leaf_inv[0, 0, :, 0], leaf_rhs[0, 0, :, 0])
        pieces = gather(leaf_yb, ex["leaf_y"])
        shaped = [mask.reshape(n_col, 1, -1) for mask in masks]
        sl = mask_tiles([sep_leaf.reshape(n_col, width, -1)], shaped[:1], width)[0].reshape(n_col * width, -1)
        blocks, leaf_col = forward_blocks(sl, pieces, ex["leaf_y"], ex["sep_sum"], width)
        top_leaf, top_sep, leaf_col = lax.optimization_barrier((top_leaf, top_sep, leaf_col))
        sums = scatter_sum(blocks, ex["sep_sum"])
        tops = [values.reshape(n_col, width, -1) for values in (top_leaf, top_sep)]
        tl, ts = [values.reshape(n_col * width, -1) for values in mask_tiles(tops, shaped[1:], width)]
        if is_direct(n_col):
            sums[0] = own_forward(sl, leaf_col, width)
        leaf_part = plain_product(tl, leaf_col, False)
        sums[0], ts, leaf_part = lax.optimization_barrier((sums[0], ts, leaf_part))
        sep_y, sep_yb = solve_forward(sums, sep_rhs[0, 0, 0], sep_inv[0, 0, 0])

        pieces = gather(sep_yb, ex["sep_y"])
        passed = swap(top_half(ts, pieces, leaf_part, ex["sep_y"], n_col, width, True), "sec", 2, 1)
        kept = top_half(ts, pieces, leaf_part, ex["sep_y"], n_col, width, False)
        sums = scatter_sum(add_sections(kept, passed, ex["top_sum"], width), ex["top_sum"])
        top_xh, top_xhb = solve_top(sums, top_rhs[0, 0], square_inverse(top_inv[0, 0]), n_col)
        top_stack = stack_pieces(gather(top_xhb, ex["top_x"]), ex["top_x"])

        blocks, top_row = top_back_blocks(ts, top_stack, swap(top_stack, "sec", 2, 1), ex["sep_t"], n_col, width)
        sums = scatter_sum(blocks, ex["sep_t"])
        if is_direct(n_row):
            sums[0] = own_back(ts, top_row, width)
        top_part = plain_product(tl, top_row, True)
        top_x = join_halves(top_xh, swap(top_xh, "sec", 2, 1), n_col)
        sep_x, sep_xb = solve_back(sums, sep_y, sep_inv[0, 0, 0])

        pieces = gather(sep_xb, ex["sep_x"])
        blocks, sep_row = back_blocks(sl, pieces, top_part, ex["sep_x"], ex["leaf_t"], span)
        sums = scatter_sum(blocks, ex["leaf_t"])
        if is_direct(n_row):
            sums[0] = own_back(sl, sep_row, span, top_part)
        leaf_x = solve_last(sums, leaf_y, split_transposes(leaf_inv[0, 0, :, 0]))
        return (
            leaf_x.reshape(1, 1, leaf_count, 1, width, cols),
            keep(sep_x)[None, None, None],
            top_x[None, None],
        )

    return body


def solution(mesh):
    in_specs = (
        P("sec", "row", None, "col", None, None),
        P("sec", "row", "col", None, None),
        P("row", "col", None, None),
        P("sec", "row", None, "col", None, None),
        P("sec", "row", "col", None, None),
        P("row", "col", None, None),
        P("sec", "row", None, None, None, None, "col", None),
        P("sec", "row", None, None, None, None, "col", None),
        P("sec", "row", None, None, None, "col", None),
        P("sec", "row", None, None, None, "col"),
        P("sec", "row", None, None, None, "col"),
        P("sec", "row", None, None, "col"),
    )
    out_specs = (
        P("sec", "row", None, "col", None, None),
        P("sec", "row", "col", None, None),
        P("row", "col", None, None),
    )
    body = make_body(mesh.shape["row"], mesh.shape["col"])
    return jax.shard_map(body, mesh=mesh, in_specs=in_specs, out_specs=out_specs, check_vma=False)
```
